128 devices in a mesh: rows: 128 (over z, x, y, core).
Axes of the slice: x: 4, y: 4, z: 4, core: 2. Of those that a mesh axis runs over, the one named last changes fastest.
Arguments:
- diag_noise: bfloat16 [1792, 128, 128], P('rows'), may hold values from -1 to 1
- couplings: bfloat16 [1792, 3, 128, 128], P('rows'), may hold values from -1 to 1
- shifts: bfloat16 [1792, 128], P('rows'), may hold values from 1.5 to 3
- near_devices: int32 [1792, 3], P('rows'), may hold values from 0 to 126, all different within a row; in each aligned block of 14 rows (0 to 13, 14 to 27, ...) at most 2 rows name the same one
- near_slots: int32 [1792, 3], P('rows'), may hold values from 0 to 13
- vectors: float32 [32, 229376], P(None, 'rows'), may hold values from -6 to 6
Outputs:
- transformed: float32 [32, 229376], P(None, 'rows')
The draws below stay inside these ranges and needn't reach their ends.
Inputs may be any that keep to these rules, and one draw needn't show every extreme that they name: `near_devices`: each row names three different distances. Among the 14 block rows of one device, no distance is named by more than 2 rows, and in some such group one distance is named by exactly 2 rows.
All inputs are finite; a program needn't handle non-finite values.
Results may differ from the reference program's by a relative error of at most 0.0014.
Values may be sent and summed in bfloat16 or wider, within the bound.
No kernel may reach another device: no remote copies, remote signals or barrier semaphores. Data moves between devices by JAX's collectives and lax.ppermute only.
A program may use at most 128 MiB of HBM per device.

```python
import math
import jax
import jax.numpy as jnp
import numpy as np
from jax import lax

BLK = 128
NVEC = 32
RB = 14
NB = 1792
PEERS = 127
CAP = 2
N_ROWS = 128


def random_signs(key, shape):
    return jnp.where(jax.random.bernoulli(key, 0.5, shape), 1.0, -1.0).astype(jnp.float32)


def draw_diag_noise(key, part):
    values = jax.random.uniform(jax.random.fold_in(key, 101), (NB, BLK, BLK), jnp.float32, -1.0, 1.0)
    signs = random_signs(jax.random.fold_in(key, 103), (NB, BLK))
    shared = signs[:, :, None] * signs[:, None, :]
    values = 0.25 * shared + 0.75 * values
    return values.astype(jnp.bfloat16)


def draw_couplings(key, part):
    values = jax.random.uniform(jax.random.fold_in(key, 201), (NB, 3, BLK, BLK), jnp.float32, -1.0, 1.0)
    row_signs = random_signs(jax.random.fold_in(key, 203), (NB, 1, BLK))
    col_signs = random_signs(jax.random.fold_in(key, 204), (NB, 3, BLK))
    shared = row_signs[:, :, :, None] * col_signs[:, :, None, :]
    values = 0.15 * shared + 0.85 * values
    return values.astype(jnp.bfloat16)


def set_ends(values, key, smallest, high):
    longest = values.shape.index(max(values.shape))
    spots = []
    for shift in (0, 1):
        where = [jax.random.randint(jax.random.fold_in(key, axis), (), 0, length) for axis, length in enumerate(values.shape)]
        where[longest] = (where[longest] + shift) % values.shape[longest]
        spots.append(tuple(where))
    return values.at[spots[0]].set(smallest).at[spots[1]].set(high)


def block_scale(key, dims, split, low, high):
    def one(dim, blocks):
        steps = jax.random.uniform(jax.random.fold_in(jax.random.fold_in(key, 6), dim), (blocks,), jnp.float32, low / len(split), high / len(split))
        return jnp.repeat(jnp.exp(steps), dims[dim] // blocks).reshape((-1,) + (1,) * (len(dims) - dim - 1))

    loudness = one(*split[0])
    for cut in split[1:]:
        loudness = loudness * one(*cut)
    return loudness


def shared_out(stream_key, own, number, rows, number_of, top, reach, slope):
    ranking = jax.random.permutation(stream_key, number_of)
    crowded, ordinary = load_shares(number_of, rows * top, reach, slope, True), load_shares(number_of, rows * top, reach, slope, False)
    places = jnp.arange(number_of)

    def named(tallies, offset_by):
        used = int((tallies > 0).sum())
        fixed = max(1, used // 4)
        passed = fixed + (places - fixed + offset_by * (used - fixed)) % max(1, number_of - fixed)
        return jnp.zeros((number_of,), jnp.int32).at[ranking[jnp.where(places < fixed, places, passed)]].set(jnp.asarray(tallies, jnp.int32))

    tallies = jnp.where(number % 4 == 0, named(crowded, number // 4), named(ordinary, number - number // 4 - 1))
    mixed = jax.random.permutation(jax.random.fold_in(own, 3), number_of)
    source_of, taker = mixed[0:number_of // 2 * 2:2], mixed[1:number_of // 2 * 2:2]
    slack = jnp.minimum(tallies[source_of] - 1, reach - tallies[taker]) // 2
    slack = jnp.where((source_of == ranking[0]) | (taker == ranking[0]) | (tallies[taker] == 0), 0, jnp.maximum(slack, 0))
    passed = jax.random.randint(jax.random.fold_in(own, 4), (number_of // 2,), 0, 1 << 20) % (slack + 1)
    tallies = tallies.at[source_of].add(-passed).at[taker].add(passed)
    members = jnp.searchsorted(jnp.cumsum(tallies), jnp.arange(rows * top), side="right").astype(jnp.int32)
    grid = members.reshape(top, rows).T
    grid = grid[jax.random.permutation(jax.random.fold_in(own, 1), rows)]
    offset_by = jax.random.randint(jax.random.fold_in(own, 2), (rows, 1), 0, top)
    return jnp.take_along_axis(grid, (jnp.arange(top)[None, :] + offset_by) % top, axis=1)


def load_shares(amount, total, limit, slope, full):
    portions = [(1 << 20) // math.isqrt(grade ** slope) + 1 for grade in range(1, amount + 1)]
    largest = limit if full else min(limit, max(-(-total // amount), total * portions[0] // sum(portions)))
    least = 1 if total - largest >= amount - 1 else 0
    given, spare = [largest] + [least] * (amount - 1), total - largest - least * (amount - 1)
    while spare > 0:
        movable = [i for i in range(1, amount) if given[i] < largest] or [i for i in range(1, amount) if given[i] < limit]
        whole, remaining = sum([portions[i] for i in movable]), spare
        for i in movable:
            addition = min(limit - given[i], max(1, remaining * portions[i] // whole), spare)
            given[i] = given[i] + addition
            spare = spare - addition
    return np.array(given)


def normal_values(key, extent, width, limit, shards=(), kind=jnp.bfloat16):
    values = jax.random.normal(key, extent, jnp.float32) * width
    if len(shards) > 0:
        values = block_scale(key, extent, shards, -0.22, 0.18) * values
    return jnp.clip(values, min=-limit, max=limit).astype(kind)


def setup_inputs(seed: int = 0) -> dict:
    splits = jax.random.split(jax.random.key(seed), 7)
    diag_noise = draw_diag_noise(jax.random.fold_in(splits[6], 71), 0)
    couplings = draw_couplings(jax.random.fold_in(splits[6], 71), 0)
    shifts = jnp.clip(jnp.exp(math.log(3.0) - 0.6931472 * jax.random.uniform(splits[2], (NB, BLK), jnp.float32) ** block_scale(splits[2], (NB, BLK), ((0, 128),), -0.2, 0.2)), 1.5, 3.0).astype(jnp.bfloat16)
    near_devices_keys = jax.random.split(jax.random.fold_in(splits[3], 1), NB // RB)
    near_devices_turns = jax.random.permutation(jax.random.fold_in(splits[3], 3), NB // RB)
    near_devices = jax.vmap(lambda own, number: shared_out(jax.random.fold_in(splits[3], 2), own, number, RB, PEERS, 3, CAP, 0))(near_devices_keys, near_devices_turns).reshape((NB, 3))
    near_slots = set_ends(jax.random.randint(splits[4], (NB, 3), 0, RB), jax.random.fold_in(splits[4], 1), 0, RB - 1).astype(jnp.int32)
    vectors = normal_values(splits[5], (NVEC, NB * BLK), 1.0, 6.0, ((1, 128),), jnp.float32)
    return dict(diag_noise=diag_noise, couplings=couplings, shifts=shifts, near_devices=near_devices, near_slots=near_slots, vectors=vectors)


highest = lax.Precision.HIGHEST

def invert(matrix):
    lower_factor = jnp.linalg.cholesky(matrix)
    identity = jnp.broadcast_to(jnp.eye(matrix.shape[-1], dtype=matrix.dtype), matrix.shape)
    inverse_lower = jax.scipy.linalg.solve_triangular(lower_factor, identity, lower=True)
    return jnp.einsum('...ba,...bc->...ac', inverse_lower, inverse_lower, precision=highest)

def build_diag(noise_block, shift_block, factor):
    noise_block = noise_block.astype(jnp.float32) * factor
    symmetric = (noise_block + jnp.swapaxes(noise_block, -1, -2)) * 0.5
    eye_block = jnp.eye(noise_block.shape[-1], dtype=jnp.float32)
    return symmetric + shift_block.astype(jnp.float32)[..., :, None] * eye_block

def row_factors(diag_own, coupling, inverse_near):
    product = jnp.einsum('rmab,rmbc->rmac', coupling, inverse_near, precision=highest)
    schur_block = diag_own - jnp.einsum('rmab,rmcb->rac', product, coupling, precision=highest)
    lower_factor = jnp.linalg.cholesky(invert(schur_block))
    factor_diag = jnp.swapaxes(lower_factor, -1, -2)
    factor_off = -jnp.einsum('rba,rmbc->rmac', lower_factor, product, precision=highest)
    return (factor_diag, factor_off)

def reference(diag_noise, couplings, shifts, near_devices, near_slots, vectors):
    factor = 0.5 / math.sqrt(BLK)
    coupling_factor = 0.4 / math.sqrt(BLK)
    owner_device = jnp.arange(NB, dtype=jnp.int32) // RB
    near_index = ((owner_device[:, None] - 1 - near_devices) % N_ROWS * RB + near_slots).astype(jnp.int32)
    inverse_all = invert(build_diag(diag_noise, shifts, factor))
    noise_spans = diag_noise.reshape(N_ROWS, RB, BLK, BLK)
    shift_spans = shifts.reshape(N_ROWS, RB, BLK)
    coupling_spans = couplings.reshape(N_ROWS, RB, 3, BLK, BLK)
    index_spans = near_index.reshape(N_ROWS, RB, 3)

    def setup_block(pieces):
        noise_block, shift_block, coupling_raw, index_block = pieces
        diag_own = build_diag(noise_block, shift_block, factor)
        coupling = coupling_raw.astype(jnp.float32) * coupling_factor
        return row_factors(diag_own, coupling, inverse_all[index_block])
    factor_diag, factor_off = lax.map(setup_block, (noise_spans, shift_spans, coupling_spans, index_spans))
    factor_diag = factor_diag.reshape(NB, BLK, BLK)
    factor_off = factor_off.reshape(NB, 3, BLK, BLK)
    vector_rows = vectors.reshape(NVEC, NB, BLK).transpose(1, 0, 2)
    left_product = jnp.einsum('rva,rab->rvb', vector_rows, factor_diag, precision=highest)
    outgoing = jnp.einsum('rva,rmab->rmvb', vector_rows, factor_off, precision=highest)
    left_product = left_product.at[near_index].add(outgoing)

    def coupling_block(pieces):
        noise_block, shift_block, coupling_raw, index_block, left_block = pieces
        diag_own = build_diag(noise_block, shift_block, factor)
        coupling = coupling_raw.astype(jnp.float32) * coupling_factor
        middle = jnp.einsum('rva,rab->rvb', left_block, diag_own, precision=highest)
        middle = middle + jnp.einsum('rmvb,rmab->rva', left_product[index_block], coupling, precision=highest)
        pushed = jnp.einsum('rva,rmab->rmvb', left_block, coupling, precision=highest)
        return (middle, pushed)
    middle_product, pushed = lax.map(coupling_block, (noise_spans, shift_spans, coupling_spans, index_spans, left_product.reshape(N_ROWS, RB, NVEC, BLK)))
    middle_product = middle_product.reshape(NB, NVEC, BLK).at[near_index].add(pushed.reshape(NB, 3, NVEC, BLK))
    result = jnp.einsum('rvb,rab->rva', middle_product, factor_diag, precision=highest)
    result = result + jnp.einsum('rmvb,rmab->rva', middle_product[near_index], factor_off, precision=highest)
    return result.transpose(1, 0, 2).reshape(NVEC, NB * BLK)
```

```python
import math

import jax
import jax.numpy as jnp
from jax import lax
from jax.experimental import pallas as pl
from jax.experimental.pallas import tpu as pltpu
from jax.sharding import PartitionSpec as P

F32 = jnp.float32
BF16 = jnp.bfloat16
BLK = 128
SLOTS = 2
TRI = 64
PAY = 80
VMEM_LIMIT = 56 * 1024 * 1024
SM = pltpu.SMEM
VM = pltpu.VMEM
highest = lax.Precision.HIGHEST


def spec(space):
    return pl.BlockSpec(memory_space=space)


def call(kernel, out_shape, ins, outs, scratch=(), flops=0, moved=0, name=None):
    return pl.pallas_call(
        kernel,
        out_shape=out_shape,
        in_specs=[spec(s) for s in ins],
        out_specs=jax.tree.map(spec, outs),
        scratch_shapes=list(scratch),
        compiler_params=pltpu.CompilerParams(vmem_limit_bytes=VMEM_LIMIT),
        cost_estimate=pl.CostEstimate(flops=flops, bytes_accessed=moved, transcendentals=0),
        name=name,
    )


def iotas(rows, lanes=BLK):
    return (
        lax.broadcasted_iota(jnp.int32, (rows, lanes), 0),
        lax.broadcasted_iota(jnp.int32, (rows, lanes), 1),
    )


def split(x):
    hi = x.astype(BF16)
    lo = (x - hi.astype(F32)).astype(BF16)
    return hi, lo


def dot(a, b, ca=1, cb=0):
    return lax.dot_general(a, b, (((ca,), (cb,)), ((), ())), preferred_element_type=F32)


def dot_exact(a, b, ca=1, cb=0):
    return lax.dot_general(
        a, b, (((ca,), (cb,)), ((), ())), preferred_element_type=F32, precision=highest
    )


def rows_times_bf16(x, b, cb=0):
    hi, lo = split(x)
    both = dot(jnp.concatenate([hi, lo], axis=0), b, 1, cb)
    n = x.shape[0]
    return both[:n] + both[n:]


def factor(z, vs, count):
    sub, lane = iotas(8)

    def panel(step, carry):
        kb = BLK // 8 - 1 - step
        row0 = pl.multiple_of(kb * 8, 8)
        part = [z[b, pl.ds(row0, 8), :] for b in range(count)]
        for j in range(7, -1, -1):
            c = row0 + j
            index = jnp.full((8, BLK), c, jnp.int32)
            at_c = lane == c
            for b in range(count):
                p = part[b]
                col = jnp.take_along_axis(p, index, axis=1, mode="promise_in_bounds")
                row = jnp.broadcast_to(p[j : j + 1, :], (8, BLK))
                d = jnp.broadcast_to(col[j : j + 1, :], (8, BLK))
                rs = lax.rsqrt(d)
                v = jnp.where(at_c, rs, row * rs)
                scaled = jnp.where(at_c, 1.0 + rs * rs, v * rs)
                vs[b, j] = scaled
                part[b] = jnp.where(sub < j, p - col * scaled, jnp.where(sub == j, v, p))
        for b in range(count):
            z[b, pl.ds(row0, 8), :] = part[b]

        def above(r, inner):
            r0 = pl.multiple_of(r * 8, 8)
            rows = [z[b, pl.ds(r0, 8), :] for b in range(count)]
            for j in range(7, -1, -1):
                index = jnp.full((8, BLK), row0 + j, jnp.int32)
                for b in range(count):
                    col = jnp.take_along_axis(rows[b], index, axis=1, mode="promise_in_bounds")
                    rows[b] = rows[b] - col * vs[b, j]
            for b in range(count):
                z[b, pl.ds(r0, 8), :] = rows[b]
            return inner

        lax.fori_loop(0, kb, above, 0)
        return carry

    lax.fori_loop(0, BLK // 8, panel, 0)


def factor_scratch(count):
    return [VM((count, BLK, BLK), F32), VM((count, 8, 8, BLK), F32)]


def build_diag(noise, shift, b, factor_value):
    sub, lane = iotas(BLK)
    n = noise[b]
    eye = (sub == lane).astype(BF16)
    turned = dot(eye, n, 1, 1)
    sym = (n.astype(F32) + turned) * (0.5 * factor_value)
    shift_row = shift[pl.ds(b, 1), :].astype(F32)
    return sym + jnp.where(sub == lane, shift_row, 0.0)


def route_kernel(me_ref, dev_ref, slot_ref, ask_ref, pos_ref, count_ref):
    n_dev = count_ref.shape[0]
    me = me_ref[0]

    def clear(t, carry):
        count_ref[t] = 0
        for r in range(SLOTS):
            ask_ref[t, r] = -1
        return carry

    lax.fori_loop(0, n_dev, clear, 0)

    def one(i, carry):
        for m in range(3):
            t = me - 1 - dev_ref[i, m]
            t = jnp.where(t < 0, t + n_dev, t)
            rank = count_ref[t]
            count_ref[t] = rank + 1
            ask_ref[t, rank] = slot_ref[i, m]
            pos_ref[i * 3 + m] = t * SLOTS + rank
        return carry

    lax.fori_loop(0, dev_ref.shape[0], one, 0)


def invert_kernel(factor_value, noise, shift, x_out, pay_out, z, vs):
    count = noise.shape[0]
    for b in range(count):
        z[b] = build_diag(noise, shift, b, factor_value)
    factor(z, vs, count)
    sub, lane = iotas(BLK)
    top_sub, top_lane = iotas(TRI)
    low_eye = (top_lane == top_sub + TRI).astype(BF16)
    diag_sub, _ = iotas(16)
    for b in range(count):
        x = jnp.where(lane >= sub, z[b], 0.0)
        x_out[b] = x
        bottom = jnp.concatenate(
            [x[TRI:].astype(BF16), jnp.zeros((TRI, BLK), BF16)], axis=0
        )
        turned = dot(low_eye, bottom, 1, 1)
        tri = jnp.where(top_lane > top_sub, x[:TRI], jnp.where(top_lane < top_sub, turned, 0.0))
        pay_out[b, :TRI, :] = tri.astype(BF16)
        diag = jnp.sum(jnp.where(sub == lane, x, 0.0), axis=0, keepdims=True)
        hi, lo = split(diag)
        tail = jnp.where(
            diag_sub == 0, hi.astype(F32), jnp.where(diag_sub == 1, lo.astype(F32), 0.0)
        )
        pay_out[b, TRI:, :] = tail.astype(BF16)


def serve_kernel(incoming, pay, out, list_pos, list_slot, list_count):
    n_dev = incoming.shape[0]
    g = pl.program_id(0)
    per = out.shape[0]

    @pl.when(g == 0)
    def _():
        list_count[0] = 0

    def one(t, carry):
        pos = g * per + t
        slot = incoming[pos // SLOTS, pos % SLOTS]

        @pl.when(slot >= 0)
        def _():
            out[t] = pay[slot]
            n = list_count[0]
            list_pos[n] = pos
            list_slot[n] = slot
            list_count[0] = n + 1

        return carry

    lax.fori_loop(0, per, one, 0)


def gram_kernel(x, e_out):
    for b in range(x.shape[0]):
        e_out[b] = dot_exact(x[b], x[b], 0, 0)


def row_kernel(
    factor_value, coupling_factor, pos, noise, shift, couplings, vectors, arrived,
    w_out, y_out, send, z, vs, near, sems,
):
    count = noise.shape[0]
    n_vec = vectors.shape[0]
    copies = []
    for q in range(3 * count):
        copy = pltpu.make_async_copy(arrived.at[pos[q]], near.at[q], sems.at[q])
        copy.start()
        copies.append(copy)
    for b in range(count):
        z[b] = build_diag(noise, shift, b, factor_value)
    for copy in copies:
        copy.wait()
    top_sub, top_lane = iotas(TRI)

    def schur(b, carry):
        total = jnp.zeros((BLK, BLK), F32)
        for m in range(3):
            q = b * 3 + m
            tri = near[q, :TRI, :].astype(F32)
            upper = jnp.where(top_lane > top_sub, tri, 0.0).astype(BF16)
            lower = jnp.where(top_lane < top_sub, tri, 0.0).astype(BF16)
            lower = pltpu.roll(lower.astype(F32), TRI, 1).astype(BF16)
            tail = near[q, TRI:, :].astype(F32)
            diag = tail[0:1] + tail[1:2]
            c = couplings[b, m]
            zero = jnp.zeros((TRI, BLK), BF16)
            y = dot(c, jnp.concatenate([upper, zero], axis=0), 1, 1)
            y = y + dot(c, jnp.concatenate([zero, lower], axis=0), 1, 0)
            y = y + c.astype(F32) * diag
            yh = y.astype(BF16)
            total = total + dot(yh, yh, 1, 1)
        z[b] = z[b] - total * (coupling_factor * coupling_factor)
        return carry

    lax.fori_loop(0, count, schur, 0)
    factor(z, vs, count)
    sub, lane = iotas(BLK)
    for b in range(count):
        w = jnp.where(lane >= sub, z[b], 0.0)
        w_out[b] = w
        y = dot_exact(vectors[:, b * BLK : (b + 1) * BLK], w)
        y_out[b] = y
        for m in range(3):
            p = rows_times_bf16(y, couplings[b, m]) * coupling_factor
            send[pos[b * 3 + m]] = p.astype(BF16)


def own_kernel(factor_value, noise, shift, y, out):
    for b in range(noise.shape[0]):
        d = build_diag(noise, shift, b, factor_value)
        out[b] = dot_exact(y[b], d)


def left_kernel(
    coupling_factor, pos, list_pos, list_slot, list_count, arrived, y, e, couplings, send, left, total
):
    count = y.shape[0]
    n_vec = y.shape[1]
    total[...] = jnp.zeros_like(total)

    def add(t, carry):
        slot = list_slot[t]
        total[slot] += arrived[list_pos[t]].astype(F32)
        return carry

    lax.fori_loop(0, list_count[0], add, 0)
    for b in range(count):
        u = dot_exact(total[b], e[b])
        left[b] = (y[b] - u).astype(BF16)
        for m in range(3):
            p = rows_times_bf16(u, couplings[b, m]) * coupling_factor
            at = pos[b * 3 + m]
            send[at // SLOTS, SLOTS + at % SLOTS] = p.astype(BF16)

    def give(t, carry):
        at = list_pos[t]
        send[at // SLOTS, at % SLOTS] = left[list_slot[t]]
        return carry

    lax.fori_loop(0, list_count[0], give, 0)


def middle_kernel(
    coupling_factor, pos, list_pos, list_slot, list_count, arrived, own, e, couplings,
    middle, send, total, answer,
):
    count = own.shape[0]
    total[...] = jnp.zeros_like(total)

    def add(t, carry):
        slot = list_slot[t]
        at = list_pos[t]
        total[slot] += arrived[at // SLOTS, SLOTS + at % SLOTS].astype(F32)
        return carry

    lax.fori_loop(0, list_count[0], add, 0)
    for b in range(count):
        near = jnp.zeros(total.shape[1:], F32)
        for m in range(3):
            at = pos[b * 3 + m]
            near = near + dot(arrived[at // SLOTS, at % SLOTS], couplings[b, m], 1, 1)
        mid = own[b] - total[b] + near * coupling_factor
        middle[b] = mid
        answer[b] = dot_exact(mid, e[b]).astype(BF16)

    def give(t, carry):
        send[list_pos[t]] = answer[list_slot[t]]
        return carry

    lax.fori_loop(0, list_count[0], give, 0)


def result_kernel(coupling_factor, pos, arrived, middle, w, couplings, out):
    for b in range(middle.shape[0]):
        near = jnp.zeros(middle.shape[1:], F32)
        for m in range(3):
            near = near + dot(arrived[pos[b * 3 + m]], couplings[b, m], 1, 1)
        mid = middle[b] - near * coupling_factor
        out[:, b * BLK : (b + 1) * BLK] = dot_exact(mid, w[b], 1, 1)


def exchange(x):
    return lax.all_to_all(x, "rows", split_axis=0, concat_axis=0, tiled=True)


def body(diag_noise, couplings, shifts, near_devices, near_slots, vectors):
    n_dev = lax.axis_size("rows")
    me = lax.axis_index("rows").astype(jnp.int32).reshape(1)
    count = diag_noise.shape[0]
    n_vec = vectors.shape[0]
    total_slots = n_dev * SLOTS
    factor_value = 0.5 / math.sqrt(BLK)
    coupling_factor = 0.4 / math.sqrt(BLK)

    def shape(dims, dtype=F32):
        return jax.ShapeDtypeStruct(dims, dtype)

    blocks = shape((count, BLK, BLK))
    rows = shape((count, n_vec, BLK))

    def with_factors(kernel, *values):
        def wrapped(*refs):
            kernel(*values, *refs)

        return wrapped

    ask, pos = call(
        route_kernel,
        (shape((n_dev, SLOTS), jnp.int32), shape((3 * count,), jnp.int32)),
        [SM, SM, SM],
        (SM, SM),
        [SM((n_dev,), jnp.int32)],
        name="route",
    )(me, near_devices, near_slots)
    incoming = exchange(ask)
    x, pay = call(
        with_factors(invert_kernel, factor_value),
        (blocks, shape((count, PAY, BLK), BF16)),
        [VM, VM],
        (VM, VM),
        factor_scratch(count),
        flops=2 * 10**9,
        moved=10**8,
        name="invert",
    )(diag_noise, shifts)
    per = 16
    answer, list_pos, list_slot, list_count = pl.pallas_call(
        serve_kernel,
        grid=(total_slots // per,),
        out_shape=(
            shape((total_slots, PAY, BLK), BF16),
            shape((total_slots,), jnp.int32),
            shape((total_slots,), jnp.int32),
            shape((1,), jnp.int32),
        ),
        in_specs=[spec(SM), spec(VM)],
        out_specs=(
            pl.BlockSpec((per, PAY, BLK), lambda g: (g, 0, 0)),
            spec(SM),
            spec(SM),
            spec(SM),
        ),
        compiler_params=pltpu.CompilerParams(
            vmem_limit_bytes=VMEM_LIMIT, dimension_semantics=("arbitrary",)
        ),
        name="serve",
    )(incoming, pay)
    arrived = exchange(answer.reshape(n_dev, SLOTS * PAY, BLK)).reshape(total_slots, PAY, BLK)
    e = call(
        gram_kernel, blocks, [VM], VM, flops=10**9, moved=10**7, name="gram"
    )(x)
    w, y, push = call(
        with_factors(row_kernel, factor_value, coupling_factor),
        (blocks, rows, shape((total_slots, n_vec, BLK), BF16)),
        [SM, VM, VM, VM, VM, pl.ANY],
        (VM, VM, VM),
        factor_scratch(count)
        + [VM((3 * count, PAY, BLK), BF16), pltpu.SemaphoreType.DMA((3 * count,))],
        name="row",
    )(pos, diag_noise, shifts, couplings, vectors, arrived)
    pushed = exchange(push.reshape(n_dev, SLOTS * n_vec, BLK)).reshape(total_slots, n_vec, BLK)
    own = call(
        with_factors(own_kernel, factor_value),
        rows, [VM, VM, VM], VM, flops=10**9, moved=10**7, name="own",
    )(diag_noise, shifts, y)
    lists = (list_pos, list_slot, list_count)
    both = call(
        with_factors(left_kernel, coupling_factor),
        shape((n_dev, 2 * SLOTS, n_vec, BLK), BF16),
        [SM] * 4 + [VM] * 4,
        VM,
        [VM((count, n_vec, BLK), BF16), VM((count, n_vec, BLK), F32)],
        name="left",
    )(pos, *lists, pushed, y, e, couplings)
    both = exchange(both.reshape(n_dev, 2 * SLOTS * n_vec, BLK)).reshape(
        n_dev, 2 * SLOTS, n_vec, BLK
    )
    middle, back = call(
        with_factors(middle_kernel, coupling_factor),
        (rows, shape((total_slots, n_vec, BLK), BF16)),
        [SM] * 4 + [VM] * 4,
        (VM, VM),
        [VM((count, n_vec, BLK), F32), VM((count, n_vec, BLK), BF16)],
        name="middle",
    )(pos, *lists, both, own, e, couplings)
    back = exchange(back.reshape(n_dev, SLOTS * n_vec, BLK)).reshape(total_slots, n_vec, BLK)
    return call(
        with_factors(result_kernel, coupling_factor),
        shape((n_vec, count * BLK)),
        [SM] + [VM] * 4,
        VM,
        name="result",
    )(pos, back, middle, w, couplings)


def solution(mesh):
    return jax.shard_map(
        body,
        mesh=mesh,
        in_specs=(
            P("rows", None, None),
            P("rows", None, None, None),
            P("rows", None),
            P("rows", None),
            P("rows", None),
            P(None, "rows"),
        ),
        out_specs=P(None, "rows"),
        check_vma=False,
    )
```

```python
import math

import jax
import jax.numpy as jnp
from jax import lax
from jax.experimental import pallas as pl
from jax.experimental.pallas import tpu as pltpu
from jax.sharding import PartitionSpec as P

F32 = jnp.float32
BF16 = jnp.bfloat16
BLK = 128
SLOTS = 2
TRI = 64
TAIL = 16
CHUNK = 2 * TRI + TAIL
SEG = 32
GROUP = BLK // SEG
CODE = 16
VMEM_LIMIT = 56 * 1024 * 1024
SM = pltpu.SMEM
VM = pltpu.VMEM
highest = lax.Precision.HIGHEST


def spec(space):
    return pl.BlockSpec(memory_space=space)


def call(kernel, out_shape, ins, outs, scratch=(), flops=0, moved=0, name=None):
    return pl.pallas_call(
        kernel,
        out_shape=out_shape,
        in_specs=[spec(s) for s in ins],
        out_specs=jax.tree.map(spec, outs),
        scratch_shapes=list(scratch),
        compiler_params=pltpu.CompilerParams(vmem_limit_bytes=VMEM_LIMIT),
        cost_estimate=pl.CostEstimate(flops=flops, bytes_accessed=moved, transcendentals=0),
        name=name,
    )


def iotas(rows, lanes=BLK):
    return (
        lax.broadcasted_iota(jnp.int32, (rows, lanes), 0),
        lax.broadcasted_iota(jnp.int32, (rows, lanes), 1),
    )


def split(x):
    hi = x.astype(BF16)
    lo = (x - hi.astype(F32)).astype(BF16)
    return hi, lo


def dot(a, b, ca=1, cb=0):
    return lax.dot_general(a, b, (((ca,), (cb,)), ((), ())), preferred_element_type=F32)


def dot_exact(a, b, ca=1, cb=0):
    return lax.dot_general(
        a, b, (((ca,), (cb,)), ((), ())), preferred_element_type=F32, precision=highest
    )


def rows_times_bf16(x, b, cb=0):
    hi, lo = split(x)
    both = dot(jnp.concatenate([hi, lo], axis=0), b, 1, cb)
    n = x.shape[0]
    return both[:n] + both[n:]


def stacked(b):
    hi, lo = split(b)
    return jnp.concatenate(
        [
            jnp.concatenate([hi, lo], axis=1),
            jnp.concatenate([hi, jnp.zeros_like(hi)], axis=1),
        ],
        axis=0,
    )


def dot_wide(a, b):
    hi, lo = split(a)
    out = dot(jnp.concatenate([hi, lo], axis=1), stacked(b))
    return out[:, :BLK] + out[:, BLK:]


def dot_rows(a, b, turned=False):
    n = a.shape[0]
    both = jnp.concatenate(split(a), axis=0)
    out = dot(both, jnp.concatenate(split(b), axis=0 if turned else 1), 1, 1 if turned else 0)
    return out[:n, :BLK] + (out[n:, :BLK] + out[:n, BLK:] + out[n:, BLK:])


def eliminate(packs):
    sub, lane = iotas(8)
    start = lane - lane % SEG
    parts = [[p[8 * t : 8 * t + 8] for t in range(SEG // 8)] for p in packs]
    for k in range(SEG - 1, -1, -1):
        i, j = divmod(k, 8)
        index = start + k
        at_k = lane == index
        for part in parts:
            row = jnp.broadcast_to(part[i][j : j + 1], (8, BLK))
            d = jnp.take_along_axis(row, index, axis=1, mode="promise_in_bounds")
            rs = lax.rsqrt(d)
            v = jnp.where(at_k, rs, row * rs)
            scaled = jnp.where(at_k, 1.0 + rs * rs, v * rs)
            for t in range(i + 1):
                if t == i and j == 0:
                    part[t] = jnp.where(sub == 0, v, part[t])
                    continue
                col = jnp.take_along_axis(part[t], index, axis=1, mode="promise_in_bounds")
                new = part[t] - col * scaled
                if t == i:
                    new = jnp.where(sub < j, new, jnp.where(sub == j, v, part[t]))
                part[t] = new
    return [jnp.concatenate(part, axis=0) for part in parts]


def factor(z, count):
    sub, lane = iotas(SEG)
    seg = lane // SEG
    groups = -(-count // GROUP)
    for kb in range(GROUP - 1, -1, -1):
        r0 = kb * SEG
        panels = [
            [z[min(q * GROUP + g, count - 1), r0 : r0 + SEG, :] for g in range(GROUP)]
            for q in range(groups)
        ]
        packs = []
        for q in range(groups):
            pack = jnp.zeros((SEG, BLK), F32)
            for g in range(GROUP):
                shift = (SEG * g - r0) % BLK
                x = panels[q][g]
                x = pltpu.roll(x, shift, 1) if shift else x
                pack = jnp.where(seg == g, x, pack)
            packs.append(pack)
        packs = eliminate(packs)
        eye = (lane - r0 == sub).astype(F32)
        for q in range(groups):
            w = jnp.where(lane % SEG >= sub, packs[q], 0.0)
            wide = jnp.concatenate([jnp.where(seg == g, w, 0.0) for g in range(GROUP)], axis=0)
            tall = jnp.concatenate(
                [jnp.where(seg == kb, eye, panels[q][g]) for g in range(GROUP)], axis=0
            )
            v = dot_wide(wide, tall)
            if kb:
                v2 = dot_wide(wide.T, v)
            for g in range(GROUP):
                b = q * GROUP + g
                if b >= count:
                    continue
                z[b, r0 : r0 + SEG, :] = v[SEG * g : SEG * g + SEG]
                if kb:
                    pads = [jnp.zeros((r0, BLK), F32), v2[SEG * g : SEG * g + SEG]]
                    if r0 + SEG < BLK:
                        pads.append(jnp.zeros((BLK - r0 - SEG, BLK), F32))
                    top = z[b, 0:r0, :]
                    update = dot_wide(top, jnp.concatenate(pads, axis=0))
                    _, top_lane = iotas(r0)
                    z[b, 0:r0, :] = jnp.where(top_lane // SEG == kb, 0.0, top) - update


def build_diag(noise, shift, b, factor_value):
    sub, lane = iotas(BLK)
    n = noise[b]
    eye = (sub == lane).astype(BF16)
    turned = dot(eye, n, 1, 1)
    sym = (n.astype(F32) + turned) * (0.5 * factor_value)
    shift_row = shift[pl.ds(b, 1), :].astype(F32)
    return sym + jnp.where(sub == lane, shift_row, 0.0)


def route_kernel(me_ref, dev_ref, slot_ref, ask_ref, pos_ref, count_ref):
    n_dev = count_ref.shape[0]
    me = me_ref[0]

    def clear(t, carry):
        count_ref[t] = 0
        ask_ref[t, 0] = 0
        return carry

    lax.fori_loop(0, n_dev, clear, 0, unroll=16)
    for i in range(dev_ref.shape[1]):
        for m in range(3):
            t = me - 1 - dev_ref[m, i]
            t = jnp.where(t < 0, t + n_dev, t)
            rank = count_ref[t]
            count_ref[t] = rank + 1
            code = slot_ref[m, i] + 1
            ask_ref[t, 0] = ask_ref[t, 0] + jnp.where(rank == 0, code, code * CODE)
            pos_ref[i * 3 + m] = t * SLOTS + rank


def list_kernel(incoming, list_pos, list_slot, list_count):
    def one(t, n):
        code = incoming[t, 0]
        for r in range(SLOTS):
            slot = (code % CODE if r == 0 else code // CODE) - 1
            list_pos[n] = t * SLOTS + r
            list_slot[n] = slot
            n = n + (slot >= 0).astype(jnp.int32)
        return n

    list_count[0] = lax.fori_loop(0, incoming.shape[0], one, 0, unroll=8)


def invert_kernel(factor_value, noise, shift, x_out, tri_out, tail_out, z):
    count = noise.shape[0]
    for b in range(count):
        z[b] = build_diag(noise, shift, b, factor_value)
    factor(z, count)
    sub, lane = iotas(BLK)
    top_sub, top_lane = iotas(TRI)
    low_eye = (top_lane == top_sub + TRI).astype(BF16)
    tail_sub, _ = iotas(TAIL)
    for b in range(count):
        x = jnp.where(lane >= sub, z[b], 0.0)
        x_out[b] = x
        bottom = jnp.concatenate([x[TRI:].astype(BF16), jnp.zeros((TRI, BLK), BF16)], axis=0)
        turned = dot(low_eye, bottom, 1, 1)
        tri = jnp.where(top_lane > top_sub, x[:TRI], jnp.where(top_lane < top_sub, turned, 0.0))
        tri_out[b] = tri.astype(BF16)
        diag = jnp.sum(jnp.where(sub == lane, x, 0.0), axis=0, keepdims=True)
        hi, lo = split(diag)
        hi, lo = hi.astype(F32), lo.astype(F32)
        for r in range(SLOTS):
            tail = jnp.where(
                tail_sub == 2 * r, hi, jnp.where(tail_sub == 2 * r + 1, lo, 0.0)
            )
            tail_out[r, b] = tail.astype(BF16)


def serve_kernel(incoming, tri, tail, out):
    per = out.shape[0]
    first = pl.program_id(0) * per
    for t in range(per):
        code = incoming[first + t, 0]
        slots = [jnp.maximum(code % CODE - 1, 0), jnp.maximum(code // CODE - 1, 0)]
        for r in range(SLOTS):
            out[t, r * TRI : (r + 1) * TRI] = tri[slots[r]]
        out[t, SLOTS * TRI :] = tail[0, slots[0]] + tail[1, slots[1]]


def gram_kernel(x, e_out):
    for b in range(x.shape[0]):
        e_out[b] = dot_exact(x[b], x[b], 0, 0)


def row_kernel(
    factor_value, coupling_factor, pos, noise, shift, couplings, vectors, arrived,
    w_out, y_out, send, z, near, tails, sems,
):
    count = noise.shape[0]
    n_vec = vectors.shape[0]
    copies = []
    for q in range(3 * count):
        at = pos[q]
        row = pl.multiple_of((at % SLOTS) * TRI, TRI)
        for k, (source, target) in enumerate(
            (
                (arrived.at[at // SLOTS, pl.ds(row, TRI)], near.at[q]),
                (arrived.at[at // SLOTS, pl.ds(SLOTS * TRI, TAIL)], tails.at[q]),
            )
        ):
            copy = pltpu.make_async_copy(source, target, sems.at[q, k])
            copy.start()
            copies.append(copy)
    for b in range(count):
        z[b] = build_diag(noise, shift, b, factor_value)
    for copy in copies:
        copy.wait()
    top_sub, top_lane = iotas(TRI)

    tail_sub, _ = iotas(TAIL)
    zero = jnp.zeros((TRI, BLK), BF16)

    def schur(b, carry):
        wide = []
        for m in range(3):
            q = b * 3 + m
            tri = near[q].astype(F32)
            upper = jnp.where(top_lane > top_sub, tri, 0.0).astype(BF16)
            lower = pltpu.roll(jnp.where(top_lane < top_sub, tri, 0.0), TRI, 1).astype(BF16)
            rank = pos[q] % SLOTS
            diag = jnp.sum(
                jnp.where(tail_sub // 2 == rank, tails[q].astype(F32), 0.0),
                axis=0,
                keepdims=True,
            )
            c = couplings[b, m]
            y = dot(c, jnp.concatenate([upper, zero], axis=0), 1, 1)
            y = y + dot(c, jnp.concatenate([zero, lower], axis=0), 1, 0)
            wide.append((y + c.astype(F32) * diag).astype(BF16))
        wide = jnp.concatenate(wide, axis=1)
        z[b] = z[b] - dot(wide, wide, 1, 1) * (coupling_factor * coupling_factor)
        return carry

    lax.fori_loop(0, count, schur, 0, unroll=2)
    factor(z, count)
    sub, lane = iotas(BLK)
    for b in range(count):
        w = jnp.where(lane >= sub, z[b], 0.0)
        w_out[b] = w
        y = dot_rows(vectors[:, b * BLK : (b + 1) * BLK], w)
        y_out[b] = y
        for m in range(3):
            p = rows_times_bf16(y, couplings[b, m]) * coupling_factor
            send[pos[b * 3 + m]] = p.astype(BF16)


def own_kernel(factor_value, noise, shift, y, out):
    for b in range(noise.shape[0]):
        d = build_diag(noise, shift, b, factor_value)
        out[b] = dot_rows(y[b], d)


def left_kernel(
    coupling_factor, pos, list_pos, list_slot, list_count, arrived, y, e, couplings, send, left, total
):
    count = y.shape[0]
    n_vec = y.shape[1]
    total[...] = jnp.zeros_like(total)

    def add(t, carry):
        slot = list_slot[t]
        total[slot] += arrived[list_pos[t]].astype(F32)
        return carry

    lax.fori_loop(0, list_count[0], add, 0)
    for b in range(count):
        u = dot_rows(total[b], e[b])
        left[b] = (y[b] - u).astype(BF16)
        for m in range(3):
            p = rows_times_bf16(u, couplings[b, m]) * coupling_factor
            at = pos[b * 3 + m]
            send[at // SLOTS, SLOTS + at % SLOTS] = p.astype(BF16)

    def give(t, carry):
        at = list_pos[t]
        send[at // SLOTS, at % SLOTS] = left[list_slot[t]]
        return carry

    lax.fori_loop(0, list_count[0], give, 0)


def middle_kernel(
    coupling_factor, pos, list_pos, list_slot, list_count, arrived, own, e, couplings,
    middle, send, total, answer,
):
    count = own.shape[0]
    total[...] = jnp.zeros_like(total)

    def add(t, carry):
        slot = list_slot[t]
        at = list_pos[t]
        total[slot] += arrived[at // SLOTS, SLOTS + at % SLOTS].astype(F32)
        return carry

    lax.fori_loop(0, list_count[0], add, 0)
    for b in range(count):
        near = jnp.zeros(total.shape[1:], F32)
        for m in range(3):
            at = pos[b * 3 + m]
            near = near + dot(arrived[at // SLOTS, at % SLOTS], couplings[b, m], 1, 1)
        mid = own[b] - total[b] + near * coupling_factor
        middle[b] = mid
        answer[b] = dot_rows(mid, e[b]).astype(BF16)

    def give(t, carry):
        send[list_pos[t]] = answer[list_slot[t]]
        return carry

    lax.fori_loop(0, list_count[0], give, 0)


def result_kernel(coupling_factor, pos, arrived, middle, w, couplings, out):
    for b in range(middle.shape[0]):
        near = jnp.zeros(middle.shape[1:], F32)
        for m in range(3):
            near = near + dot(arrived[pos[b * 3 + m]], couplings[b, m], 1, 1)
        mid = middle[b] - near * coupling_factor
        out[:, b * BLK : (b + 1) * BLK] = dot_rows(mid, w[b], True)


def exchange(x):
    return lax.all_to_all(x, "rows", split_axis=0, concat_axis=0, tiled=True)


def body(diag_noise, couplings, shifts, near_devices, near_slots, vectors):
    n_dev = lax.axis_size("rows")
    me = lax.axis_index("rows").astype(jnp.int32).reshape(1)
    count = diag_noise.shape[0]
    n_vec = vectors.shape[0]
    total_slots = n_dev * SLOTS
    factor_value = 0.5 / math.sqrt(BLK)
    coupling_factor = 0.4 / math.sqrt(BLK)

    def shape(dims, dtype=F32):
        return jax.ShapeDtypeStruct(dims, dtype)

    blocks = shape((count, BLK, BLK))
    rows = shape((count, n_vec, BLK))

    def with_factors(kernel, *values):
        def wrapped(*refs):
            kernel(*values, *refs)

        return wrapped

    ask, pos = call(
        route_kernel,
        (shape((n_dev, 1), jnp.int32), shape((3 * count,), jnp.int32)),
        [SM, SM, SM],
        (SM, SM),
        [SM((n_dev,), jnp.int32)],
        name="route",
    )(me, near_devices.T, near_slots.T)
    incoming = exchange(ask)
    x, tri, tail = call(
        with_factors(invert_kernel, factor_value),
        (
            blocks,
            shape((count, TRI, BLK), BF16),
            shape((SLOTS, count, TAIL, BLK), BF16),
        ),
        [VM, VM],
        (VM, VM, VM),
        [VM((count, BLK, BLK), F32)],
        flops=2 * 10**9,
        moved=10**8,
        name="invert",
    )(diag_noise, shifts)
    per = 16
    answer = pl.pallas_call(
        serve_kernel,
        grid=(n_dev // per,),
        out_shape=shape((n_dev, CHUNK, BLK), BF16),
        in_specs=[spec(SM), spec(VM), spec(VM)],
        out_specs=pl.BlockSpec((per, CHUNK, BLK), lambda g: (g, 0, 0)),
        compiler_params=pltpu.CompilerParams(dimension_semantics=("arbitrary",)),
        name="serve",
    )(incoming, tri, tail)
    arrived = exchange(answer)
    lists = call(
        list_kernel,
        (
            shape((total_slots + SLOTS,), jnp.int32),
            shape((total_slots + SLOTS,), jnp.int32),
            shape((1,), jnp.int32),
        ),
        [SM],
        (SM, SM, SM),
        flops=10**9,
        moved=10**7,
        name="list",
    )(incoming)
    e = call(
        gram_kernel, blocks, [VM], VM, flops=10**9, moved=10**7, name="gram"
    )(x)
    w, y, push = call(
        with_factors(row_kernel, factor_value, coupling_factor),
        (blocks, rows, shape((total_slots, n_vec, BLK), BF16)),
        [SM, VM, VM, VM, VM, pl.ANY],
        (VM, VM, VM),
        [
            VM((count, BLK, BLK), F32),
            VM((3 * count, TRI, BLK), BF16),
            VM((3 * count, TAIL, BLK), BF16),
            pltpu.SemaphoreType.DMA((3 * count, 2)),
        ],
        name="row",
    )(pos, diag_noise, shifts, couplings, vectors, arrived)
    pushed = exchange(push.reshape(n_dev, SLOTS * n_vec, BLK)).reshape(total_slots, n_vec, BLK)
    own = call(
        with_factors(own_kernel, factor_value),
        rows, [VM, VM, VM], VM, flops=10**9, moved=10**7, name="own",
    )(diag_noise, shifts, y)
    both = call(
        with_factors(left_kernel, coupling_factor),
        shape((n_dev, 2 * SLOTS, n_vec, BLK), BF16),
        [SM] * 4 + [VM] * 4,
        VM,
        [VM((count, n_vec, BLK), BF16), VM((count, n_vec, BLK), F32)],
        name="left",
    )(pos, *lists, pushed, y, e, couplings)
    both = exchange(both.reshape(n_dev, 2 * SLOTS * n_vec, BLK)).reshape(
        n_dev, 2 * SLOTS, n_vec, BLK
    )
    middle, back = call(
        with_factors(middle_kernel, coupling_factor),
        (rows, shape((total_slots, n_vec, BLK), BF16)),
        [SM] * 4 + [VM] * 4,
        (VM, VM),
        [VM((count, n_vec, BLK), F32), VM((count, n_vec, BLK), BF16)],
        name="middle",
    )(pos, *lists, both, own, e, couplings)
    back = exchange(back.reshape(n_dev, SLOTS * n_vec, BLK)).reshape(total_slots, n_vec, BLK)
    return call(
        with_factors(result_kernel, coupling_factor),
        shape((n_vec, count * BLK)),
        [SM] + [VM] * 4,
        VM,
        name="result",
    )(pos, back, middle, w, couplings)


def solution(mesh):
    return jax.shard_map(
        body,
        mesh=mesh,
        in_specs=(
            P("rows", None, None),
            P("rows", None, None, None),
            P("rows", None),
            P("rows", None),
            P("rows", None),
            P(None, "rows"),
        ),
        out_specs=P(None, "rows"),
        check_vma=False,
    )
```

```python
import math

import jax
import jax.numpy as jnp
from jax import lax
from jax.experimental import pallas as pl
from jax.experimental.pallas import tpu as pltpu
from jax.sharding import PartitionSpec as P

F32 = jnp.float32
BF16 = jnp.bfloat16
BLK = 128
SLOTS = 2
TRI = 64
TAIL = 16
CHUNK = 2 * TRI + TAIL
SEG = 32
GROUP = BLK // SEG
CODE = 16
VMEM_LIMIT = 16 * 1024 * 1024
SM = pltpu.SMEM
VM = pltpu.VMEM
highest = lax.Precision.HIGHEST


def spec(space):
    return pl.BlockSpec(memory_space=space)


def call(kernel, out_shape, ins, outs, scratch=(), flops=0, moved=0, name=None):
    return pl.pallas_call(
        kernel,
        out_shape=out_shape,
        in_specs=[spec(s) for s in ins],
        out_specs=jax.tree.map(spec, outs),
        scratch_shapes=list(scratch),
        compiler_params=pltpu.CompilerParams(vmem_limit_bytes=VMEM_LIMIT),
        cost_estimate=pl.CostEstimate(flops=flops, bytes_accessed=moved, transcendentals=0),
        name=name,
    )


def iotas(rows, lanes=BLK):
    return (
        lax.broadcasted_iota(jnp.int32, (rows, lanes), 0),
        lax.broadcasted_iota(jnp.int32, (rows, lanes), 1),
    )


def split(x):
    hi = x.astype(BF16)
    lo = (x - hi.astype(F32)).astype(BF16)
    return hi, lo


def dot(a, b, ca=1, cb=0):
    return lax.dot_general(a, b, (((ca,), (cb,)), ((), ())), preferred_element_type=F32)


def dot_exact(a, b, ca=1, cb=0):
    return lax.dot_general(
        a, b, (((ca,), (cb,)), ((), ())), preferred_element_type=F32, precision=highest
    )


def rows_times_bf16(x, b, cb=0):
    hi, lo = split(x)
    both = dot(jnp.concatenate([hi, lo], axis=0), b, 1, cb)
    n = x.shape[0]
    return both[:n] + both[n:]


def stacked(b):
    hi, lo = split(b)
    return jnp.concatenate(
        [
            jnp.concatenate([hi, lo], axis=1),
            jnp.concatenate([hi, jnp.zeros_like(hi)], axis=1),
        ],
        axis=0,
    )


def dot_wide(a, b):
    hi, lo = split(a)
    out = dot(jnp.concatenate([hi, lo], axis=1), stacked(b))
    return out[:, :BLK] + out[:, BLK:]


def dot_rows(a, b, turned=False):
    n = a.shape[0]
    both = jnp.concatenate(split(a), axis=0)
    out = dot(both, jnp.concatenate(split(b), axis=0 if turned else 1), 1, 1 if turned else 0)
    return out[:n, :BLK] + (out[n:, :BLK] + out[:n, BLK:] + out[n:, BLK:])


def eliminate(packs):
    sub, lane = iotas(8)
    start = lane - lane % SEG
    parts = [[p[8 * t : 8 * t + 8] for t in range(SEG // 8)] for p in packs]
    for k in range(SEG - 1, -1, -1):
        i, j = divmod(k, 8)
        index = start + k
        at_k = lane == index
        for part in parts:
            row = jnp.broadcast_to(part[i][j : j + 1], (8, BLK))
            d = jnp.take_along_axis(row, index, axis=1, mode="promise_in_bounds")
            rs = lax.rsqrt(d)
            v = jnp.where(at_k, rs, row * rs)
            scaled = jnp.where(at_k, 1.0 + rs * rs, v * rs)
            for t in range(i + 1):
                if t == i and j == 0:
                    part[t] = jnp.where(sub == 0, v, part[t])
                    continue
                col = jnp.take_along_axis(part[t], index, axis=1, mode="promise_in_bounds")
                new = part[t] - col * scaled
                if t == i:
                    new = jnp.where(sub < j, new, jnp.where(sub == j, v, part[t]))
                part[t] = new
    return [jnp.concatenate(part, axis=0) for part in parts]


def factor(z, count):
    sub, lane = iotas(SEG)
    seg = lane // SEG
    groups = -(-count // GROUP)
    for kb in range(GROUP - 1, -1, -1):
        r0 = kb * SEG
        panels = [
            [z[min(q * GROUP + g, count - 1), r0 : r0 + SEG, :] for g in range(GROUP)]
            for q in range(groups)
        ]
        packs = []
        for q in range(groups):
            pack = jnp.zeros((SEG, BLK), F32)
            for g in range(GROUP):
                shift = (SEG * g - r0) % BLK
                x = panels[q][g]
                x = pltpu.roll(x, shift, 1) if shift else x
                pack = jnp.where(seg == g, x, pack)
            packs.append(pack)
        packs = eliminate(packs)
        eye = (lane - r0 == sub).astype(F32)
        for q in range(groups):
            w = jnp.where(lane % SEG >= sub, packs[q], 0.0)
            wide = jnp.concatenate([jnp.where(seg == g, w, 0.0) for g in range(GROUP)], axis=0)
            tall = jnp.concatenate(
                [jnp.where(seg == kb, eye, panels[q][g]) for g in range(GROUP)], axis=0
            )
            v = dot_wide(wide, tall)
            if kb:
                v2 = dot_wide(wide.T, v)
            for g in range(GROUP):
                b = q * GROUP + g
                if b >= count:
                    continue
                z[b, r0 : r0 + SEG, :] = v[SEG * g : SEG * g + SEG]
                if kb:
                    pads = [jnp.zeros((r0, BLK), F32), v2[SEG * g : SEG * g + SEG]]
                    if r0 + SEG < BLK:
                        pads.append(jnp.zeros((BLK - r0 - SEG, BLK), F32))
                    top = z[b, 0:r0, :]
                    update = dot_wide(top, jnp.concatenate(pads, axis=0))
                    _, top_lane = iotas(r0)
                    z[b, 0:r0, :] = jnp.where(top_lane // SEG == kb, 0.0, top) - update


def build_diag(noise, shift, b, factor_value):
    sub, lane = iotas(BLK)
    n = noise[b]
    eye = (sub == lane).astype(BF16)
    turned = dot(eye, n, 1, 1)
    sym = (n.astype(F32) + turned) * (0.5 * factor_value)
    shift_row = shift[pl.ds(b, 1), :].astype(F32)
    return sym + jnp.where(sub == lane, shift_row, 0.0)


def route_kernel(me_ref, dev_ref, slot_ref, ask_ref, pos_ref, count_ref):
    n_dev = count_ref.shape[0]
    me = me_ref[0]

    def clear(t, carry):
        count_ref[t] = 0
        ask_ref[t, 0] = 0
        return carry

    lax.fori_loop(0, n_dev, clear, 0, unroll=16)
    for i in range(dev_ref.shape[1]):
        for m in range(3):
            t = me - 1 - dev_ref[m, i]
            t = jnp.where(t < 0, t + n_dev, t)
            rank = count_ref[t]
            count_ref[t] = rank + 1
            code = slot_ref[m, i] + 1
            ask_ref[t, 0] = ask_ref[t, 0] + jnp.where(rank == 0, code, code * CODE)
            pos_ref[i * 3 + m] = t * SLOTS + rank


def list_kernel(incoming, list_pos, list_slot, list_count):
    def one(t, n):
        code = incoming[t, 0]
        for r in range(SLOTS):
            slot = (code % CODE if r == 0 else code // CODE) - 1
            list_pos[n] = t * SLOTS + r
            list_slot[n] = slot
            n = n + (slot >= 0).astype(jnp.int32)
        return n

    list_count[0] = lax.fori_loop(0, incoming.shape[0], one, 0, unroll=8)


def invert_kernel(factor_value, noise, shift, x_out, tri_out, tail_out, z):
    count = noise.shape[0]
    for b in range(count):
        z[b] = build_diag(noise, shift, b, factor_value)
    factor(z, count)
    sub, lane = iotas(BLK)
    top_sub, top_lane = iotas(TRI)
    low_eye = (top_lane == top_sub + TRI).astype(BF16)
    tail_sub, _ = iotas(TAIL)
    for b in range(count):
        x = jnp.where(lane >= sub, z[b], 0.0)
        x_out[b] = x
        bottom = jnp.concatenate([x[TRI:].astype(BF16), jnp.zeros((TRI, BLK), BF16)], axis=0)
        turned = dot(low_eye, bottom, 1, 1)
        tri = jnp.where(top_lane > top_sub, x[:TRI], jnp.where(top_lane < top_sub, turned, 0.0))
        tri_out[b] = tri.astype(BF16)
        diag = jnp.sum(jnp.where(sub == lane, x, 0.0), axis=0, keepdims=True)
        hi, lo = split(diag)
        hi, lo = hi.astype(F32), lo.astype(F32)
        for r in range(SLOTS):
            tail = jnp.where(
                tail_sub == 2 * r, hi, jnp.where(tail_sub == 2 * r + 1, lo, 0.0)
            )
            tail_out[r, b] = tail.astype(BF16)


def serve_kernel(incoming, tri, tail, out):
    def one(t, carry):
        code = incoming[t, 0]
        slots = [jnp.maximum(code % CODE - 1, 0), jnp.maximum(code // CODE - 1, 0)]
        for r in range(SLOTS):
            out[t, r * TRI : (r + 1) * TRI] = tri[slots[r]]
        out[t, SLOTS * TRI :] = tail[0, slots[0]] + tail[1, slots[1]]
        return carry

    lax.fori_loop(0, out.shape[0], one, 0, unroll=8)


def gram_kernel(x, e_out):
    for b in range(x.shape[0]):
        e_out[b] = dot_exact(x[b], x[b], 0, 0)


def row_kernel(
    factor_value, coupling_factor, pos, noise, shift, couplings, vectors, arrived,
    w_out, y_out, send, z,
):
    count = noise.shape[0]
    n_vec = vectors.shape[0]
    for b in range(count):
        z[b] = build_diag(noise, shift, b, factor_value)
    top_sub, top_lane = iotas(TRI)

    tail_sub, _ = iotas(TAIL)
    zero = jnp.zeros((TRI, BLK), BF16)

    def schur(b, carry):
        wide = []
        for m in range(3):
            q = b * 3 + m
            at = pos[q]
            dev, rank = at // SLOTS, at % SLOTS
            first = pl.multiple_of(rank * TRI, TRI)
            tri = arrived[dev, pl.ds(first, TRI), :].astype(F32)
            upper = jnp.where(top_lane > top_sub, tri, 0.0).astype(BF16)
            lower = pltpu.roll(jnp.where(top_lane < top_sub, tri, 0.0), TRI, 1).astype(BF16)
            diag = jnp.sum(
                jnp.where(tail_sub // 2 == rank, arrived[dev, SLOTS * TRI :, :].astype(F32), 0.0),
                axis=0,
                keepdims=True,
            )
            c = couplings[b, m]
            y = dot(c, jnp.concatenate([upper, zero], axis=0), 1, 1)
            y = y + dot(c, jnp.concatenate([zero, lower], axis=0), 1, 0)
            wide.append((y + c.astype(F32) * diag).astype(BF16))
        wide = jnp.concatenate(wide, axis=1)
        z[b] = z[b] - dot(wide, wide, 1, 1) * (coupling_factor * coupling_factor)
        return carry

    lax.fori_loop(0, count, schur, 0, unroll=2)
    factor(z, count)
    sub, lane = iotas(BLK)
    for b in range(count):
        w = jnp.where(lane >= sub, z[b], 0.0)
        w_out[b] = w
        y = dot_rows(vectors[:, b * BLK : (b + 1) * BLK], w)
        y_out[b] = y
        for m in range(3):
            p = rows_times_bf16(y, couplings[b, m]) * coupling_factor
            send[pos[b * 3 + m]] = p.astype(BF16)


def own_kernel(factor_value, noise, shift, y, out):
    for b in range(noise.shape[0]):
        d = build_diag(noise, shift, b, factor_value)
        out[b] = dot_rows(y[b], d)


def left_kernel(
    coupling_factor, pos, list_pos, list_slot, list_count, arrived, y, e, couplings, send, left, total
):
    count = y.shape[0]
    n_vec = y.shape[1]
    total[...] = jnp.zeros_like(total)

    def add(t, carry):
        slot = list_slot[t]
        total[slot] += arrived[list_pos[t]].astype(F32)
        return carry

    lax.fori_loop(0, list_count[0], add, 0)
    for b in range(count):
        u = dot_rows(total[b], e[b])
        left[b] = (y[b] - u).astype(BF16)
        for m in range(3):
            p = rows_times_bf16(u, couplings[b, m]) * coupling_factor
            at = pos[b * 3 + m]
            send[at // SLOTS, SLOTS + at % SLOTS] = p.astype(BF16)

    def give(t, carry):
        at = list_pos[t]
        send[at // SLOTS, at % SLOTS] = left[list_slot[t]]
        return carry

    lax.fori_loop(0, list_count[0], give, 0)


def middle_kernel(
    coupling_factor, pos, list_pos, list_slot, list_count, arrived, own, e, couplings,
    middle, send, total, answer,
):
    count = own.shape[0]
    total[...] = jnp.zeros_like(total)

    def add(t, carry):
        slot = list_slot[t]
        at = list_pos[t]
        total[slot] += arrived[at // SLOTS, SLOTS + at % SLOTS].astype(F32)
        return carry

    lax.fori_loop(0, list_count[0], add, 0)
    for b in range(count):
        near = jnp.zeros(total.shape[1:], F32)
        for m in range(3):
            at = pos[b * 3 + m]
            near = near + dot(arrived[at // SLOTS, at % SLOTS], couplings[b, m], 1, 1)
        mid = own[b] - total[b] + near * coupling_factor
        middle[b] = mid
        answer[b] = dot_rows(mid, e[b]).astype(BF16)

    def give(t, carry):
        send[list_pos[t]] = answer[list_slot[t]]
        return carry

    lax.fori_loop(0, list_count[0], give, 0)


def result_kernel(coupling_factor, pos, arrived, middle, w, couplings, out):
    for b in range(middle.shape[0]):
        near = jnp.zeros(middle.shape[1:], F32)
        for m in range(3):
            near = near + dot(arrived[pos[b * 3 + m]], couplings[b, m], 1, 1)
        mid = middle[b] - near * coupling_factor
        out[:, b * BLK : (b + 1) * BLK] = dot_rows(mid, w[b], True)


def exchange(x):
    return lax.all_to_all(x, "rows", split_axis=0, concat_axis=0, tiled=True)


def body(diag_noise, couplings, shifts, near_devices, near_slots, vectors):
    n_dev = lax.axis_size("rows")
    me = lax.axis_index("rows").astype(jnp.int32).reshape(1)
    count = diag_noise.shape[0]
    n_vec = vectors.shape[0]
    total_slots = n_dev * SLOTS
    factor_value = 0.5 / math.sqrt(BLK)
    coupling_factor = 0.4 / math.sqrt(BLK)

    def shape(dims, dtype=F32):
        return jax.ShapeDtypeStruct(dims, dtype)

    blocks = shape((count, BLK, BLK))
    rows = shape((count, n_vec, BLK))

    def with_factors(kernel, *values):
        def wrapped(*refs):
            kernel(*values, *refs)

        return wrapped

    ask, pos = call(
        route_kernel,
        (shape((n_dev, 1), jnp.int32), shape((3 * count,), jnp.int32)),
        [SM, SM, SM],
        (SM, SM),
        [SM((n_dev,), jnp.int32)],
        name="route",
    )(me, near_devices.T, near_slots.T)
    incoming = exchange(ask)
    x, tri, tail = call(
        with_factors(invert_kernel, factor_value),
        (
            blocks,
            shape((count, TRI, BLK), BF16),
            shape((SLOTS, count, TAIL, BLK), BF16),
        ),
        [VM, VM],
        (VM, VM, VM),
        [VM((count, BLK, BLK), F32)],
        flops=2 * 10**9,
        moved=10**8,
        name="invert",
    )(diag_noise, shifts)
    answer = call(
        serve_kernel,
        shape((n_dev, CHUNK, BLK), BF16),
        [SM, VM, VM],
        VM,
        name="serve",
    )(incoming, tri, tail)
    arrived = exchange(answer)
    lists = call(
        list_kernel,
        (
            shape((total_slots + SLOTS,), jnp.int32),
            shape((total_slots + SLOTS,), jnp.int32),
            shape((1,), jnp.int32),
        ),
        [SM],
        (SM, SM, SM),
        flops=10**9,
        moved=10**7,
        name="list",
    )(incoming)
    e = call(
        gram_kernel, blocks, [VM], VM, flops=10**9, moved=10**7, name="gram"
    )(x)
    w, y, push = call(
        with_factors(row_kernel, factor_value, coupling_factor),
        (blocks, rows, shape((total_slots, n_vec, BLK), BF16)),
        [SM, VM, VM, VM, VM, VM],
        (VM, VM, VM),
        [VM((count, BLK, BLK), F32)],
        name="row",
    )(pos, diag_noise, shifts, couplings, vectors, arrived)
    pushed = exchange(push.reshape(n_dev, SLOTS * n_vec, BLK)).reshape(total_slots, n_vec, BLK)
    own = call(
        with_factors(own_kernel, factor_value),
        rows, [VM, VM, VM], VM, flops=10**9, moved=10**7, name="own",
    )(diag_noise, shifts, y)
    both = call(
        with_factors(left_kernel, coupling_factor),
        shape((n_dev, 2 * SLOTS, n_vec, BLK), BF16),
        [SM] * 4 + [VM] * 4,
        VM,
        [VM((count, n_vec, BLK), BF16), VM((count, n_vec, BLK), F32)],
        name="left",
    )(pos, *lists, pushed, y, e, couplings)
    both = exchange(both.reshape(n_dev, 2 * SLOTS * n_vec, BLK)).reshape(
        n_dev, 2 * SLOTS, n_vec, BLK
    )
    middle, back = call(
        with_factors(middle_kernel, coupling_factor),
        (rows, shape((total_slots, n_vec, BLK), BF16)),
        [SM] * 4 + [VM] * 4,
        (VM, VM),
        [VM((count, n_vec, BLK), F32), VM((count, n_vec, BLK), BF16)],
        name="middle",
    )(pos, *lists, both, own, e, couplings)
    back = exchange(back.reshape(n_dev, SLOTS * n_vec, BLK)).reshape(total_slots, n_vec, BLK)
    return call(
        with_factors(result_kernel, coupling_factor),
        shape((n_vec, count * BLK)),
        [SM] + [VM] * 4,
        VM,
        name="result",
    )(pos, back, middle, w, couplings)


def solution(mesh):
    return jax.shard_map(
        body,
        mesh=mesh,
        in_specs=(
            P("rows", None, None),
            P("rows", None, None, None),
            P("rows", None),
            P("rows", None),
            P("rows", None),
            P(None, "rows"),
        ),
        out_specs=P(None, "rows"),
        check_vma=False,
    )
```

```python
import math

import jax
import jax.numpy as jnp
from jax import lax
from jax.experimental import pallas as pl
from jax.experimental.pallas import tpu as pltpu
from jax.sharding import PartitionSpec as P

F32 = jnp.float32
BF16 = jnp.bfloat16
BLK = 128
SLOTS = 2
TRI = 64
TAIL = 16
CHUNK = 2 * TRI + TAIL
SEG = 16
STEP = 8
GROUP = BLK // SEG
CODE = 16
VMEM_LIMIT = 16 * 1024 * 1024
SM = pltpu.SMEM
VM = pltpu.VMEM
highest = lax.Precision.HIGHEST


def spec(space):
    return pl.BlockSpec(memory_space=space)


def call(kernel, out_shape, ins, outs, scratch=(), flops=0, moved=0, name=None):
    return pl.pallas_call(
        kernel,
        out_shape=out_shape,
        in_specs=[spec(s) for s in ins],
        out_specs=jax.tree.map(spec, outs),
        scratch_shapes=list(scratch),
        compiler_params=pltpu.CompilerParams(vmem_limit_bytes=VMEM_LIMIT),
        cost_estimate=pl.CostEstimate(flops=flops, bytes_accessed=moved, transcendentals=0),
        name=name,
    )


def iotas(rows, lanes=BLK):
    return (
        lax.broadcasted_iota(jnp.int32, (rows, lanes), 0),
        lax.broadcasted_iota(jnp.int32, (rows, lanes), 1),
    )


def split(x):
    hi = x.astype(BF16)
    lo = (x - hi.astype(F32)).astype(BF16)
    return hi, lo


def dot(a, b, ca=1, cb=0):
    return lax.dot_general(a, b, (((ca,), (cb,)), ((), ())), preferred_element_type=F32)


def dot_exact(a, b, ca=1, cb=0):
    return lax.dot_general(
        a, b, (((ca,), (cb,)), ((), ())), preferred_element_type=F32, precision=highest
    )


def rows_times_bf16(x, b, cb=0):
    hi, lo = split(x)
    both = dot(jnp.concatenate([hi, lo], axis=0), b, 1, cb)
    n = x.shape[0]
    return both[:n] + both[n:]


def stacked(b):
    hi, lo = split(b)
    return jnp.concatenate(
        [
            jnp.concatenate([hi, lo], axis=1),
            jnp.concatenate([hi, jnp.zeros_like(hi)], axis=1),
        ],
        axis=0,
    )


def dot_wide(a, b):
    hi, lo = split(a)
    out = dot(jnp.concatenate([hi, lo], axis=1), stacked(b))
    return out[:, :BLK] + out[:, BLK:]


def pair(b, axis):
    return jnp.concatenate(split(b), axis=axis)


def dot_pair(a, b, cb=0):
    n = a.shape[0]
    out = dot(pair(a, 0), b, 1, cb)
    return out[:n, :BLK] + (out[n:, :BLK] + out[:n, BLK:] + out[n:, BLK:])


def side_by_side(c, b):
    return jnp.concatenate([c[b, m] for m in range(3)], axis=1)


def eliminate(packs):
    sub, lane = iotas(8)
    start = lane - lane % SEG
    parts = [[p[8 * t : 8 * t + 8] for t in range(SEG // 8)] for p in packs]
    for k in range(SEG - 1, -1, -STEP):
        i = k // 8
        spots = [k % 8 - b for b in range(STEP)]
        index = [start + (k - b) for b in range(STEP)]
        at = [lane == x for x in index]
        for part in parts:
            cols = [
                [jnp.take_along_axis(part[t], x, axis=1, mode="promise_in_bounds") for x in index]
                for t in range(i + 1)
            ]
            pivot = [
                [jnp.broadcast_to(c[spots[b] : spots[b] + 1], (8, BLK)) for c in cols[i]]
                for b in range(STEP)
            ]
            ratio = [[None] * STEP for _ in range(STEP)]
            final, scaled = [], []
            for b in range(STEP):
                row = jnp.broadcast_to(part[i][spots[b] : spots[b] + 1], (8, BLK))
                for a in range(b):
                    row = row - pivot[a][b] * scaled[a]
                    for c in range(b, STEP):
                        pivot[b][c] = pivot[b][c] - ratio[a][b] * pivot[a][c]
                root = lax.rsqrt(pivot[b][b])
                inverse = root * root
                for c in range(b + 1, STEP):
                    ratio[b][c] = inverse * pivot[b][c]
                final.append(jnp.where(at[b], root, row * root))
                scaled.append(jnp.where(at[b], 1.0 + inverse, row * inverse))
            for t in range(i):
                new = part[t]
                for b in range(STEP):
                    col = cols[t][b]
                    for a in range(b):
                        col = col - cols[t][a] * ratio[a][b]
                    cols[t][b] = col
                    new = new - col * scaled[b]
                part[t] = new
            for b in range(STEP):
                part[i] = jnp.where(sub == spots[b], final[b], part[i])
    return [jnp.concatenate(part, axis=0) for part in parts]


def factor(z, count):
    sub, lane = iotas(SEG)
    seg = lane // SEG
    groups = -(-count // GROUP)
    for kb in range(GROUP - 1, -1, -1):
        r0 = kb * SEG
        panels = [
            [z[min(q * GROUP + g, count - 1), r0 : r0 + SEG, :] for g in range(GROUP)]
            for q in range(groups)
        ]
        packs = []
        for q in range(groups):
            pack = jnp.zeros((SEG, BLK), F32)
            for g in range(GROUP):
                shift = (SEG * g - r0) % BLK
                x = panels[q][g]
                x = pltpu.roll(x, shift, 1) if shift else x
                pack = jnp.where(seg == g, x, pack)
            packs.append(pack)
        packs = eliminate(packs)
        eye = (lane - r0 == sub).astype(F32)
        for q in range(groups):
            w = jnp.where(lane % SEG >= sub, packs[q], 0.0)
            wide = jnp.concatenate([jnp.where(seg == g, w, 0.0) for g in range(GROUP)], axis=0)
            tall = jnp.concatenate(
                [jnp.where(seg == kb, eye, panels[q][g]) for g in range(GROUP)], axis=0
            )
            v = dot_wide(wide, tall)
            if kb:
                v2 = dot_wide(wide.T, v)
            for g in range(GROUP):
                b = q * GROUP + g
                if b >= count:
                    continue
                z[b, r0 : r0 + SEG, :] = v[SEG * g : SEG * g + SEG]
                if kb:
                    pads = [jnp.zeros((r0, BLK), F32), v2[SEG * g : SEG * g + SEG]]
                    if r0 + SEG < BLK:
                        pads.append(jnp.zeros((BLK - r0 - SEG, BLK), F32))
                    top = z[b, 0:r0, :]
                    update = dot_wide(top, jnp.concatenate(pads, axis=0))
                    _, top_lane = iotas(r0)
                    z[b, 0:r0, :] = jnp.where(top_lane // SEG == kb, 0.0, top) - update


def build_diag(noise, shift, b, factor_value):
    sub, lane = iotas(BLK)
    n = noise[b]
    eye = (sub == lane).astype(BF16)
    turned = dot(eye, n, 1, 1)
    sym = (n.astype(F32) + turned) * (0.5 * factor_value)
    shift_row = shift[pl.ds(b, 1), :].astype(F32)
    return sym + jnp.where(sub == lane, shift_row, 0.0)


def route_kernel(me_ref, dev_ref, slot_ref, ask_ref, pos_ref, count_ref):
    n_dev = count_ref.shape[0]
    me = me_ref[0]

    def clear(t, carry):
        count_ref[t] = 0
        ask_ref[t, 0] = 0
        return carry

    lax.fori_loop(0, n_dev, clear, 0, unroll=16)
    for i in range(dev_ref.shape[1]):
        for m in range(3):
            t = me - 1 - dev_ref[m, i]
            t = jnp.where(t < 0, t + n_dev, t)
            rank = count_ref[t]
            count_ref[t] = rank + 1
            code = slot_ref[m, i] + 1
            ask_ref[t, 0] = ask_ref[t, 0] + jnp.where(rank == 0, code, code * CODE)
            pos_ref[i * 3 + m] = t * SLOTS + rank


def list_kernel(incoming, list_pos, list_slot, list_count):
    def one(t, n):
        code = incoming[t, 0]
        for r in range(SLOTS):
            slot = (code % CODE if r == 0 else code // CODE) - 1
            list_pos[n] = t * SLOTS + r
            list_slot[n] = slot
            n = n + (slot >= 0).astype(jnp.int32)
        return n

    list_count[0] = lax.fori_loop(0, incoming.shape[0], one, 0, unroll=8)


def invert_kernel(factor_value, noise, shift, x_out, tri_out, tail_out, z):
    count = noise.shape[0]
    for b in range(count):
        z[b] = build_diag(noise, shift, b, factor_value)
    factor(z, count)
    sub, lane = iotas(BLK)
    top_sub, top_lane = iotas(TRI)
    low_eye = (top_lane == top_sub + TRI).astype(BF16)
    tail_sub, _ = iotas(TAIL)
    for b in range(count):
        x = jnp.where(lane >= sub, z[b], 0.0)
        x_out[b] = x
        bottom = jnp.concatenate([x[TRI:].astype(BF16), jnp.zeros((TRI, BLK), BF16)], axis=0)
        turned = dot(low_eye, bottom, 1, 1)
        tri = jnp.where(top_lane > top_sub, x[:TRI], jnp.where(top_lane < top_sub, turned, 0.0))
        tri_out[b] = tri.astype(BF16)
        diag = jnp.sum(jnp.where(sub == lane, x, 0.0), axis=0, keepdims=True)
        hi, lo = split(diag)
        hi, lo = hi.astype(F32), lo.astype(F32)
        for r in range(SLOTS):
            tail = jnp.where(
                tail_sub == 2 * r, hi, jnp.where(tail_sub == 2 * r + 1, lo, 0.0)
            )
            tail_out[r, b] = tail.astype(BF16)


def serve_kernel(incoming, tri, tail, out):
    def one(t, carry):
        code = incoming[t, 0]
        slots = [jnp.maximum(code % CODE - 1, 0), jnp.maximum(code // CODE - 1, 0)]
        for r in range(SLOTS):
            out[t, r * TRI : (r + 1) * TRI] = tri[slots[r]]
        out[t, SLOTS * TRI :] = tail[0, slots[0]] + tail[1, slots[1]]
        return carry

    lax.fori_loop(0, out.shape[0], one, 0, unroll=8)


def gram_kernel(x, e_out):
    for b in range(x.shape[0]):
        e_out[b] = pair(dot_exact(x[b], x[b], 0, 0), 1)


def row_kernel(
    factor_value, coupling_factor, pos, noise, shift, couplings, vectors, arrived,
    w_out, y_out, send, z, stage, sems,
):
    count = noise.shape[0]
    n_vec = vectors.shape[0]
    for b in range(count):
        z[b] = build_diag(noise, shift, b, factor_value)
    top_sub, top_lane = iotas(TRI)

    tail_sub, _ = iotas(TAIL)
    zero = jnp.zeros((TRI, BLK), BF16)

    def schur(b, carry):
        wide = []
        for m in range(3):
            q = b * 3 + m
            at = pos[q]
            dev, rank = at // SLOTS, at % SLOTS
            first = pl.multiple_of(rank * TRI, TRI)
            tri = arrived[dev, pl.ds(first, TRI), :].astype(F32)
            upper = jnp.where(top_lane > top_sub, tri, 0.0).astype(BF16)
            lower = pltpu.roll(jnp.where(top_lane < top_sub, tri, 0.0), TRI, 1).astype(BF16)
            diag = jnp.sum(
                jnp.where(tail_sub // 2 == rank, arrived[dev, SLOTS * TRI :, :].astype(F32), 0.0),
                axis=0,
                keepdims=True,
            )
            c = couplings[b, m]
            y = dot(c, jnp.concatenate([upper, zero], axis=0), 1, 1)
            y = y + dot(c, jnp.concatenate([zero, lower], axis=0), 1, 0)
            wide.append((y + c.astype(F32) * diag).astype(BF16))
        wide = jnp.concatenate(wide, axis=1)
        z[b] = z[b] - dot(wide, wide, 1, 1) * (coupling_factor * coupling_factor)
        return carry

    lax.fori_loop(0, count, schur, 0, unroll=2)
    factor(z, count)
    sub, lane = iotas(BLK)
    copies = []
    for b in range(count):
        w = jnp.where(lane >= sub, z[b], 0.0)
        hi, lo = split(w)
        w_out[b] = jnp.concatenate([hi, lo], axis=0)
        y = dot_pair(vectors[:, b * BLK : (b + 1) * BLK], jnp.concatenate([hi, lo], axis=1))
        y_out[b] = y
        p = (rows_times_bf16(y, side_by_side(couplings, b)) * coupling_factor).astype(BF16)
        for m in range(3):
            q = b * 3 + m
            stage[q] = p[:, m * BLK : (m + 1) * BLK]
            copy = pltpu.make_async_copy(stage.at[q], send.at[pos[q]], sems.at[q])
            copy.start()
            copies.append(copy)
    for copy in copies:
        copy.wait()


def own_kernel(factor_value, noise, shift, y, out):
    for b in range(noise.shape[0]):
        d = build_diag(noise, shift, b, factor_value)
        out[b] = dot_pair(y[b], pair(d, 1))


def left_kernel(
    coupling_factor, pos, list_pos, list_slot, list_count, arrived, y, e, couplings, send,
    left, total, stage, sems, give_sems,
):
    count = y.shape[0]
    n_vec = y.shape[1]
    total[...] = jnp.zeros_like(total)

    def add(t, carry):
        slot = list_slot[t]
        total[slot] += arrived[list_pos[t]].astype(F32)
        return carry

    lax.fori_loop(0, list_count[0], add, 0)
    copies = []
    for b in range(count):
        u = dot_pair(total[b], e[b])
        left[b] = (y[b] - u).astype(BF16)
        p = (rows_times_bf16(u, side_by_side(couplings, b)) * coupling_factor).astype(BF16)
        for m in range(3):
            q = b * 3 + m
            at = pos[q]
            stage[q] = p[:, m * BLK : (m + 1) * BLK]
            copy = pltpu.make_async_copy(
                stage.at[q], send.at[at // SLOTS, SLOTS + at % SLOTS], sems.at[q]
            )
            copy.start()
            copies.append(copy)

    def gift(t):
        at = list_pos[t]
        return pltpu.make_async_copy(
            left.at[list_slot[t]], send.at[at // SLOTS, at % SLOTS], give_sems.at[t]
        )

    def give(t, carry):
        gift(t).start()
        return carry

    def finish(t, carry):
        gift(t).wait()
        return carry

    lax.fori_loop(0, list_count[0], give, 0)
    for copy in copies:
        copy.wait()
    lax.fori_loop(0, list_count[0], finish, 0)


def middle_kernel(
    coupling_factor, pos, list_pos, list_slot, list_count, arrived, own, e, couplings,
    middle, send, total, answer,
):
    count = own.shape[0]
    total[...] = jnp.zeros_like(total)

    def add(t, carry):
        slot = list_slot[t]
        at = list_pos[t]
        total[slot] += arrived[at // SLOTS, SLOTS + at % SLOTS].astype(F32)
        return carry

    lax.fori_loop(0, list_count[0], add, 0)
    for b in range(count):
        places = [pos[b * 3 + m] for m in range(3)]
        near = jnp.concatenate([arrived[at // SLOTS, at % SLOTS] for at in places], axis=1)
        near = dot(near, side_by_side(couplings, b), 1, 1)
        mid = own[b] - total[b] + near * coupling_factor
        middle[b] = mid
        answer[b] = dot_pair(mid, e[b]).astype(BF16)

    def give(t, carry):
        send[list_pos[t]] = answer[list_slot[t]]
        return carry

    lax.fori_loop(0, list_count[0], give, 0)


def result_kernel(coupling_factor, pos, arrived, middle, w, couplings, out):
    for b in range(middle.shape[0]):
        near = jnp.concatenate([arrived[pos[b * 3 + m]] for m in range(3)], axis=1)
        near = dot(near, side_by_side(couplings, b), 1, 1)
        mid = middle[b] - near * coupling_factor
        out[:, b * BLK : (b + 1) * BLK] = dot_pair(mid, w[b], 1)


def exchange(x):
    return lax.all_to_all(x, "rows", split_axis=0, concat_axis=0, tiled=True)


def body(diag_noise, couplings, shifts, near_devices, near_slots, vectors):
    n_dev = lax.axis_size("rows")
    me = lax.axis_index("rows").astype(jnp.int32).reshape(1)
    count = diag_noise.shape[0]
    n_vec = vectors.shape[0]
    total_slots = n_dev * SLOTS
    factor_value = 0.5 / math.sqrt(BLK)
    coupling_factor = 0.4 / math.sqrt(BLK)

    def shape(dims, dtype=F32):
        return jax.ShapeDtypeStruct(dims, dtype)

    blocks = shape((count, BLK, BLK))
    rows = shape((count, n_vec, BLK))

    def with_factors(kernel, *values):
        def wrapped(*refs):
            kernel(*values, *refs)

        return wrapped

    ask, pos = call(
        route_kernel,
        (shape((n_dev, 1), jnp.int32), shape((3 * count,), jnp.int32)),
        [SM, SM, SM],
        (SM, SM),
        [SM((n_dev,), jnp.int32)],
        name="route",
    )(me, near_devices.T, near_slots.T)
    incoming = exchange(ask)
    x, tri, tail = call(
        with_factors(invert_kernel, factor_value),
        (
            blocks,
            shape((count, TRI, BLK), BF16),
            shape((SLOTS, count, TAIL, BLK), BF16),
        ),
        [VM, VM],
        (VM, VM, VM),
        [VM((count, BLK, BLK), F32)],
        flops=2 * 10**9,
        moved=10**8,
        name="invert",
    )(diag_noise, shifts)
    answer = call(
        serve_kernel,
        shape((n_dev, CHUNK, BLK), BF16),
        [SM, VM, VM],
        VM,
        name="serve",
    )(incoming, tri, tail)
    arrived = exchange(answer)
    lists = call(
        list_kernel,
        (
            shape((total_slots + SLOTS,), jnp.int32),
            shape((total_slots + SLOTS,), jnp.int32),
            shape((1,), jnp.int32),
        ),
        [SM],
        (SM, SM, SM),
        flops=10**9,
        moved=10**7,
        name="list",
    )(incoming)
    e = call(
        gram_kernel, shape((count, BLK, 2 * BLK), BF16), [VM], VM, flops=10**9, moved=10**7, name="gram"
    )(x)
    w, y, push = call(
        with_factors(row_kernel, factor_value, coupling_factor),
        (shape((count, 2 * BLK, BLK), BF16), rows, pltpu.HBM((total_slots, n_vec, BLK), BF16)),
        [SM, VM, VM, VM, VM, VM],
        (VM, VM, pltpu.HBM),
        [
            VM((count, BLK, BLK), F32),
            VM((3 * count, n_vec, BLK), BF16),
            pltpu.SemaphoreType.DMA((3 * count,)),
        ],
        name="row",
    )(pos, diag_noise, shifts, couplings, vectors, arrived)
    pushed = exchange(push.reshape(n_dev, SLOTS * n_vec, BLK)).reshape(total_slots, n_vec, BLK)
    own = call(
        with_factors(own_kernel, factor_value),
        rows, [VM, VM, VM], VM, flops=10**9, moved=10**7, name="own",
    )(diag_noise, shifts, y)
    both = call(
        with_factors(left_kernel, coupling_factor),
        pltpu.HBM((n_dev, 2 * SLOTS, n_vec, BLK), BF16),
        [SM] * 4 + [VM] * 4,
        pltpu.HBM,
        [
            VM((count, n_vec, BLK), BF16),
            VM((count, n_vec, BLK), F32),
            VM((3 * count, n_vec, BLK), BF16),
            pltpu.SemaphoreType.DMA((3 * count,)),
            pltpu.SemaphoreType.DMA((total_slots,)),
        ],
        name="left",
    )(pos, *lists, pushed, y, e, couplings)
    both = exchange(both.reshape(n_dev, 2 * SLOTS * n_vec, BLK)).reshape(
        n_dev, 2 * SLOTS, n_vec, BLK
    )
    middle, back = call(
        with_factors(middle_kernel, coupling_factor),
        (rows, shape((total_slots, n_vec, BLK), BF16)),
        [SM] * 4 + [VM] * 4,
        (VM, VM),
        [VM((count, n_vec, BLK), F32), VM((count, n_vec, BLK), BF16)],
        name="middle",
    )(pos, *lists, both, own, e, couplings)
    back = exchange(back.reshape(n_dev, SLOTS * n_vec, BLK)).reshape(total_slots, n_vec, BLK)
    return call(
        with_factors(result_kernel, coupling_factor),
        shape((n_vec, count * BLK)),
        [SM] + [VM] * 4,
        VM,
        name="result",
    )(pos, back, middle, w, couplings)


def solution(mesh):
    return jax.shard_map(
        body,
        mesh=mesh,
        in_specs=(
            P("rows", None, None),
            P("rows", None, None, None),
            P("rows", None),
            P("rows", None),
            P("rows", None),
            P(None, "rows"),
        ),
        out_specs=P(None, "rows"),
        check_vma=False,
    )
```

```python
import functools
import math

import jax
import jax.numpy as jnp
from jax import lax
from jax.experimental import pallas as pl
from jax.experimental.pallas import tpu as pltpu
from jax.sharding import PartitionSpec as P

F32 = jnp.float32
BF16 = jnp.bfloat16
BLK = 128
SLOTS = 2
TRI = 64
TAIL = 16
CHUNK = 2 * TRI + TAIL
SEG = 16
STEP = 8
GROUP = BLK // SEG
CODE = 16
VMEM_LIMIT = 16 * 1024 * 1024
SM = pltpu.SMEM
VM = pltpu.VMEM
highest = lax.Precision.HIGHEST


def spec(space):
    return pl.BlockSpec(memory_space=space)


def call(kernel, out_shape, ins, outs, scratch=(), flops=0, moved=0, name=None):
    return pl.pallas_call(
        kernel,
        out_shape=out_shape,
        in_specs=[spec(s) for s in ins],
        out_specs=jax.tree.map(spec, outs),
        scratch_shapes=list(scratch),
        compiler_params=pltpu.CompilerParams(vmem_limit_bytes=VMEM_LIMIT),
        cost_estimate=pl.CostEstimate(flops=flops, bytes_accessed=moved, transcendentals=0),
        name=name,
    )


def iotas(rows, lanes=BLK):
    return (
        lax.broadcasted_iota(jnp.int32, (rows, lanes), 0),
        lax.broadcasted_iota(jnp.int32, (rows, lanes), 1),
    )


def split(x):
    hi = x.astype(BF16)
    lo = (x - hi.astype(F32)).astype(BF16)
    return hi, lo


def dot(a, b, ca=1, cb=0):
    return lax.dot_general(a, b, (((ca,), (cb,)), ((), ())), preferred_element_type=F32)


def dot_exact(a, b, ca=1, cb=0):
    return lax.dot_general(
        a, b, (((ca,), (cb,)), ((), ())), preferred_element_type=F32, precision=highest
    )


def rows_times_bf16(x, b, cb=0):
    hi, lo = split(x)
    both = dot(jnp.concatenate([hi, lo], axis=0), b, 1, cb)
    n = x.shape[0]
    return both[:n] + both[n:]


def stacked(b):
    hi, lo = split(b)
    return jnp.concatenate(
        [
            jnp.concatenate([hi, lo], axis=1),
            jnp.concatenate([hi, jnp.zeros_like(hi)], axis=1),
        ],
        axis=0,
    )


def dot_wide(a, b):
    hi, lo = split(a)
    out = dot(jnp.concatenate([hi, lo], axis=1), stacked(b))
    return out[:, :BLK] + out[:, BLK:]


def pair(b, axis):
    return jnp.concatenate(split(b), axis=axis)


def dot_pair(a, b, cb=0):
    n = a.shape[0]
    out = dot(pair(a, 0), b, 1, cb)
    return out[:n, :BLK] + (out[n:, :BLK] + out[:n, BLK:] + out[n:, BLK:])


def side_by_side(c, b):
    return jnp.concatenate([c[b, m] for m in range(3)], axis=1)


def eliminate(packs):
    sub, lane = iotas(8)
    start = lane - lane % SEG
    parts = [[p[8 * t : 8 * t + 8] for t in range(SEG // 8)] for p in packs]
    for k in range(SEG - 1, -1, -STEP):
        i = k // 8
        spots = [k % 8 - b for b in range(STEP)]
        index = [start + (k - b) for b in range(STEP)]
        at = [lane == x for x in index]
        for part in parts:
            cols = [
                [jnp.take_along_axis(part[t], x, axis=1, mode="promise_in_bounds") for x in index]
                for t in range(i + 1)
            ]
            pivot = [
                [jnp.broadcast_to(c[spots[b] : spots[b] + 1], (8, BLK)) for c in cols[i]]
                for b in range(STEP)
            ]
            ratio = [[None] * STEP for _ in range(STEP)]
            final, scaled = [], []
            for b in range(STEP):
                row = jnp.broadcast_to(part[i][spots[b] : spots[b] + 1], (8, BLK))
                for a in range(b):
                    row = row - pivot[a][b] * scaled[a]
                    for c in range(b, STEP):
                        pivot[b][c] = pivot[b][c] - ratio[a][b] * pivot[a][c]
                root = lax.rsqrt(pivot[b][b])
                inverse = root * root
                for c in range(b + 1, STEP):
                    ratio[b][c] = inverse * pivot[b][c]
                final.append(jnp.where(at[b], root, row * root))
                scaled.append(jnp.where(at[b], 1.0 + inverse, row * inverse))
            for t in range(i):
                new = part[t]
                for b in range(STEP):
                    col = cols[t][b]
                    for a in range(b):
                        col = col - cols[t][a] * ratio[a][b]
                    cols[t][b] = col
                    new = new - col * scaled[b]
                part[t] = new
            for b in range(STEP):
                part[i] = jnp.where(sub == spots[b], final[b], part[i])
    return [jnp.concatenate(part, axis=0) for part in parts]


def factor(z, count):
    sub, lane = iotas(SEG)
    seg = lane // SEG
    groups = -(-count // GROUP)
    for kb in range(GROUP - 1, -1, -1):
        r0 = kb * SEG
        panels = [
            [z[min(q * GROUP + g, count - 1), r0 : r0 + SEG, :] for g in range(GROUP)]
            for q in range(groups)
        ]
        packs = []
        for q in range(groups):
            pack = jnp.zeros((SEG, BLK), F32)
            for g in range(GROUP):
                shift = (SEG * g - r0) % BLK
                x = panels[q][g]
                x = pltpu.roll(x, shift, 1) if shift else x
                pack = jnp.where(seg == g, x, pack)
            packs.append(pack)
        packs = eliminate(packs)
        eye = (lane - r0 == sub).astype(F32)
        for q in range(groups):
            w = jnp.where(lane % SEG >= sub, packs[q], 0.0)
            wide = jnp.concatenate([jnp.where(seg == g, w, 0.0) for g in range(GROUP)], axis=0)
            tall = jnp.concatenate(
                [jnp.where(seg == kb, eye, panels[q][g]) for g in range(GROUP)], axis=0
            )
            v = dot_wide(wide, tall)
            if kb:
                v2 = dot_wide(wide.T, v)
            for g in range(GROUP):
                b = q * GROUP + g
                if b >= count:
                    continue
                z[b, r0 : r0 + SEG, :] = v[SEG * g : SEG * g + SEG]
                if kb:
                    pads = [jnp.zeros((r0, BLK), F32), v2[SEG * g : SEG * g + SEG]]
                    if r0 + SEG < BLK:
                        pads.append(jnp.zeros((BLK - r0 - SEG, BLK), F32))
                    top = z[b, 0:r0, :]
                    update = dot_wide(top, jnp.concatenate(pads, axis=0))
                    _, top_lane = iotas(r0)
                    z[b, 0:r0, :] = jnp.where(top_lane // SEG == kb, 0.0, top) - update


def build_diag(noise, shift, b, factor_value):
    sub, lane = iotas(BLK)
    n = noise[b]
    eye = (sub == lane).astype(BF16)
    turned = dot(eye, n, 1, 1)
    sym = (n.astype(F32) + turned) * (0.5 * factor_value)
    shift_row = shift[pl.ds(b, 1), :].astype(F32)
    return sym + jnp.where(sub == lane, shift_row, 0.0)


def route_kernel(me_ref, dev_ref, slot_ref, ask_ref, pos_ref, count_ref):
    n_dev = count_ref.shape[0]
    me = me_ref[0]

    def clear(t, carry):
        count_ref[t] = 0
        return carry

    lax.fori_loop(0, n_dev, clear, 0, unroll=32)
    _, lane = iotas(8, n_dev)
    codes = jnp.zeros((8, n_dev), jnp.int32)
    for i in range(dev_ref.shape[1]):
        for m in range(3):
            t = me - 1 - dev_ref[m, i]
            t = jnp.where(t < 0, t + n_dev, t)
            rank = count_ref[t]
            count_ref[t] = rank + 1
            code = slot_ref[m, i] + 1
            code = jnp.where(rank == 0, code, code * CODE)
            codes = codes + jnp.where(lane == t, code, 0)
            pos_ref[i * 3 + m] = t * SLOTS + rank
    for t in range(n_dev // 8):
        ask_ref[8 * t : 8 * t + 8, :] = codes


def invert_kernel(factor_value, noise, shift, x_out, tri_out, tail_out, z):
    count = noise.shape[0]
    for b in range(count):
        z[b] = build_diag(noise, shift, b, factor_value)
    factor(z, count)
    sub, lane = iotas(BLK)
    top_sub, top_lane = iotas(TRI)
    low_eye = (top_lane == top_sub + TRI).astype(BF16)
    tail_sub, _ = iotas(TAIL)
    for b in range(count):
        x = jnp.where(lane >= sub, z[b], 0.0)
        x_out[b] = x
        bottom = jnp.concatenate([x[TRI:].astype(BF16), jnp.zeros((TRI, BLK), BF16)], axis=0)
        turned = dot(low_eye, bottom, 1, 1)
        tri = jnp.where(top_lane > top_sub, x[:TRI], jnp.where(top_lane < top_sub, turned, 0.0))
        tri_out[b] = tri.astype(BF16)
        diag = jnp.sum(jnp.where(sub == lane, x, 0.0), axis=0, keepdims=True)
        hi, lo = split(diag)
        hi, lo = hi.astype(F32), lo.astype(F32)
        for r in range(SLOTS):
            tail = jnp.where(
                tail_sub == 2 * r, hi, jnp.where(tail_sub == 2 * r + 1, lo, 0.0)
            )
            tail_out[r, b] = tail.astype(BF16)


def serve_kernel(me_ref, incoming, tri, tail, out):
    me = me_ref[0]

    def one(t, carry):
        code = incoming[t, me]
        slots = [jnp.maximum(code % CODE - 1, 0), jnp.maximum(code // CODE - 1, 0)]
        for r in range(SLOTS):
            out[t, r * TRI : (r + 1) * TRI] = tri[slots[r]]
        out[t, SLOTS * TRI :] = tail[0, slots[0]] + tail[1, slots[1]]
        return carry

    lax.fori_loop(0, out.shape[0], one, 0, unroll=8)


def row_kernel(
    factor_value, coupling_factor, pos, noise, shift, couplings, vectors, arrived,
    w_out, y_out, send, z, stage, sems,
):
    count = noise.shape[0]
    n_vec = vectors.shape[0]
    for b in range(count):
        z[b] = build_diag(noise, shift, b, factor_value)
    top_sub, top_lane = iotas(TRI)

    tail_sub, _ = iotas(TAIL)
    zero = jnp.zeros((TRI, BLK), BF16)

    def schur(b, carry):
        wide = []
        for m in range(3):
            q = b * 3 + m
            at = pos[q]
            dev, rank = at // SLOTS, at % SLOTS
            first = pl.multiple_of(rank * TRI, TRI)
            tri = arrived[dev, pl.ds(first, TRI), :].astype(F32)
            upper = jnp.where(top_lane > top_sub, tri, 0.0).astype(BF16)
            lower = pltpu.roll(jnp.where(top_lane < top_sub, tri, 0.0), TRI, 1).astype(BF16)
            diag = jnp.sum(
                jnp.where(tail_sub // 2 == rank, arrived[dev, SLOTS * TRI :, :].astype(F32), 0.0),
                axis=0,
                keepdims=True,
            )
            c = couplings[b, m]
            y = dot(c, jnp.concatenate([upper, zero], axis=0), 1, 1)
            y = y + dot(c, jnp.concatenate([zero, lower], axis=0), 1, 0)
            wide.append((y + c.astype(F32) * diag).astype(BF16))
        wide = jnp.concatenate(wide, axis=1)
        z[b] = z[b] - dot(wide, wide, 1, 1) * (coupling_factor * coupling_factor)
        return carry

    lax.fori_loop(0, count, schur, 0, unroll=2)
    factor(z, count)
    sub, lane = iotas(BLK)
    copies = []
    for b in range(count):
        w = jnp.where(lane >= sub, z[b], 0.0)
        hi, lo = split(w)
        w_out[b] = jnp.concatenate([hi, lo], axis=0)
        y = dot_pair(vectors[:, b * BLK : (b + 1) * BLK], jnp.concatenate([hi, lo], axis=1))
        y_out[b] = y
        p = (rows_times_bf16(y, side_by_side(couplings, b)) * coupling_factor).astype(BF16)
        for m in range(3):
            q = b * 3 + m
            stage[q] = p[:, m * BLK : (m + 1) * BLK]
            copy = pltpu.make_async_copy(stage.at[q], send.at[pos[q]], sems.at[q])
            copy.start()
            copies.append(copy)
    for copy in copies:
        copy.wait()


def between_kernel(
    factor_value, me_ref, incoming, table, x, noise, shift, y,
    e_out, own_out, list_pos, list_slot, list_count, clash,
):
    me = me_ref[0]

    def one(t, n):
        code = incoming[t, me]
        for r in range(SLOTS):
            slot = (code % CODE if r == 0 else code // CODE) - 1
            list_pos[n] = t * SLOTS + r
            list_slot[n] = slot
            n = n + (slot >= 0).astype(jnp.int32)
        return n

    list_count[0] = lax.fori_loop(0, incoming.shape[0], one, 0, unroll=8)
    double = (table[...] >= CODE).astype(F32)
    clash[0] = (jnp.max(double * double.T) > 0.5).astype(jnp.int32)
    for b in range(noise.shape[0]):
        e_out[b] = pair(dot_exact(x[b], x[b], 0, 0), 1)
        d = build_diag(noise, shift, b, factor_value)
        own_out[b] = dot_pair(y[b], pair(d, 1))


def push_slot(slots, rank):
    return SLOTS + rank if slots == 2 * SLOTS else SLOTS - rank


def left_kernel(
    coupling_factor, pos, list_pos, list_slot, list_count, arrived, y, e, couplings, send, left, total
):
    count = y.shape[0]
    total[...] = jnp.zeros_like(total)

    def add(t, carry):
        slot = list_slot[t]
        total[slot] += arrived[list_pos[t]].astype(F32)
        return carry

    lax.fori_loop(0, list_count[0], add, 0)
    for b in range(count):
        u = dot_pair(total[b], e[b])
        left[b] = (y[b] - u).astype(BF16)
        p = (rows_times_bf16(u, side_by_side(couplings, b)) * coupling_factor).astype(BF16)
        for m in range(3):
            at = pos[b * 3 + m]
            send[at // SLOTS, push_slot(send.shape[1], at % SLOTS)] = p[:, m * BLK : (m + 1) * BLK]

    def give(t, carry):
        at = list_pos[t]
        send[at // SLOTS, at % SLOTS] = left[list_slot[t]]
        return carry

    lax.fori_loop(0, list_count[0], give, 0)


def middle_kernel(
    coupling_factor, pos, list_pos, list_slot, list_count, arrived, own, e, couplings,
    middle, send, total, answer,
):
    count = own.shape[0]
    total[...] = jnp.zeros_like(total)

    def add(t, carry):
        slot = list_slot[t]
        at = list_pos[t]
        place = push_slot(arrived.shape[1], at % SLOTS)
        total[slot] += arrived[at // SLOTS, place].astype(F32)
        return carry

    lax.fori_loop(0, list_count[0], add, 0)
    for b in range(count):
        places = [pos[b * 3 + m] for m in range(3)]
        near = jnp.concatenate([arrived[at // SLOTS, at % SLOTS] for at in places], axis=1)
        near = dot(near, side_by_side(couplings, b), 1, 1)
        mid = own[b] - total[b] + near * coupling_factor
        middle[b] = mid
        answer[b] = dot_pair(mid, e[b]).astype(BF16)

    def give(t, carry):
        send[list_pos[t]] = answer[list_slot[t]]
        return carry

    lax.fori_loop(0, list_count[0], give, 0)


def result_kernel(coupling_factor, pos, arrived, middle, w, couplings, out):
    for b in range(middle.shape[0]):
        near = jnp.concatenate([arrived[pos[b * 3 + m]] for m in range(3)], axis=1)
        near = dot(near, side_by_side(couplings, b), 1, 1)
        mid = middle[b] - near * coupling_factor
        out[:, b * BLK : (b + 1) * BLK] = dot_pair(mid, w[b], 1)


def exchange(x):
    return lax.all_to_all(x, "rows", split_axis=0, concat_axis=0, tiled=True)


def body(diag_noise, couplings, shifts, near_devices, near_slots, vectors):
    n_dev = lax.axis_size("rows")
    me = lax.axis_index("rows").astype(jnp.int32).reshape(1)
    count = diag_noise.shape[0]
    n_vec = vectors.shape[0]
    total_slots = n_dev * SLOTS
    factor_value = 0.5 / math.sqrt(BLK)
    coupling_factor = 0.4 / math.sqrt(BLK)

    def shape(dims, dtype=F32):
        return jax.ShapeDtypeStruct(dims, dtype)

    blocks = shape((count, BLK, BLK))
    rows = shape((count, n_vec, BLK))

    def with_factors(kernel, *values):
        def wrapped(*refs):
            kernel(*values, *refs)

        return wrapped

    ask, pos = call(
        route_kernel,
        (shape((n_dev, n_dev), jnp.int32), shape((3 * count,), jnp.int32)),
        [SM, SM, SM],
        (VM, SM),
        [SM((n_dev,), jnp.int32)],
        name="route",
    )(me, near_devices.T, near_slots.T)
    table = exchange(ask)
    x, tri, tail = call(
        with_factors(invert_kernel, factor_value),
        (
            blocks,
            shape((count, TRI, BLK), BF16),
            shape((SLOTS, count, TAIL, BLK), BF16),
        ),
        [VM, VM],
        (VM, VM, VM),
        [VM((count, BLK, BLK), F32)],
        flops=2 * 10**9,
        moved=10**8,
        name="invert",
    )(diag_noise, shifts)
    answer = call(
        serve_kernel,
        shape((n_dev, CHUNK, BLK), BF16),
        [SM, SM, VM, VM],
        VM,
        name="serve",
    )(me, table, tri, tail)
    arrived = exchange(answer)
    w, y, push = call(
        with_factors(row_kernel, factor_value, coupling_factor),
        (shape((count, 2 * BLK, BLK), BF16), rows, pltpu.HBM((total_slots, n_vec, BLK), BF16)),
        [SM, VM, VM, VM, VM, VM],
        (VM, VM, pltpu.HBM),
        [
            VM((count, BLK, BLK), F32),
            VM((3 * count, n_vec, BLK), BF16),
            pltpu.SemaphoreType.DMA((3 * count,)),
        ],
        name="row",
    )(pos, diag_noise, shifts, couplings, vectors, arrived)
    pushed = exchange(push.reshape(n_dev, SLOTS * n_vec, BLK)).reshape(total_slots, n_vec, BLK)
    e, own, *lists, clash = call(
        with_factors(between_kernel, factor_value),
        (
            shape((count, BLK, 2 * BLK), BF16),
            rows,
            shape((total_slots + SLOTS,), jnp.int32),
            shape((total_slots + SLOTS,), jnp.int32),
            shape((1,), jnp.int32),
            shape((1,), jnp.int32),
        ),
        [SM, SM] + [VM] * 5,
        (VM, VM, SM, SM, SM, SM),
        flops=2 * 10**9,
        moved=10**7,
        name="between",
    )(me, table, table, x, diag_noise, shifts, y)

    def swap(slots, pos, lists, pushed, y, e, own, couplings):
        both = call(
            with_factors(left_kernel, coupling_factor),
            shape((n_dev, slots, n_vec, BLK), BF16),
            [SM] * 4 + [VM] * 4,
            VM,
            [VM((count, n_vec, BLK), BF16), VM((count, n_vec, BLK), F32)],
            name="left",
        )(pos, *lists, pushed, y, e, couplings)
        both = exchange(both.reshape(n_dev, slots * n_vec, BLK)).reshape(
            n_dev, slots, n_vec, BLK
        )
        return call(
            with_factors(middle_kernel, coupling_factor),
            (rows, shape((total_slots, n_vec, BLK), BF16)),
            [SM] * 4 + [VM] * 4,
            (VM, VM),
            [VM((count, n_vec, BLK), F32), VM((count, n_vec, BLK), BF16)],
            name="middle",
        )(pos, *lists, both, own, e, couplings)

    middle, back = lax.cond(
        clash[0] > 0,
        functools.partial(swap, 2 * SLOTS),
        functools.partial(swap, 2 * SLOTS - 1),
        pos, lists, pushed, y, e, own, couplings,
    )
    back = exchange(back.reshape(n_dev, SLOTS * n_vec, BLK)).reshape(total_slots, n_vec, BLK)
    return call(
        with_factors(result_kernel, coupling_factor),
        shape((n_vec, count * BLK)),
        [SM] + [VM] * 4,
        VM,
        name="result",
    )(pos, back, middle, w, couplings)


def solution(mesh):
    return jax.shard_map(
        body,
        mesh=mesh,
        in_specs=(
            P("rows", None, None),
            P("rows", None, None, None),
            P("rows", None),
            P("rows", None),
            P("rows", None),
            P(None, "rows"),
        ),
        out_specs=P(None, "rows"),
        check_vma=False,
    )
```

```python
import functools
import math

import jax
import jax.numpy as jnp
from jax import lax
from jax.experimental import pallas as pl
from jax.experimental.pallas import tpu as pltpu
from jax.sharding import PartitionSpec as P

F32 = jnp.float32
BF16 = jnp.bfloat16
BLK = 128
SLOTS = 2
CORES = 2
TRI = 64
TAIL = 16
HALF = TRI // 2
PAY = TRI + SLOTS * TAIL
SEG = 16
STEP = 8
GROUP = BLK // SEG
CODE = 16
VMEM_LIMIT = 16 * 1024 * 1024
SM = pltpu.SMEM
VM = pltpu.VMEM
highest = lax.Precision.HIGHEST


def spec(space):
    return pl.BlockSpec(memory_space=space)


def call(kernel, out_shape, ins, outs, scratch=(), flops=0, moved=0, name=None):
    return pl.pallas_call(
        kernel,
        out_shape=out_shape,
        in_specs=[spec(s) for s in ins],
        out_specs=jax.tree.map(spec, outs),
        scratch_shapes=list(scratch),
        compiler_params=pltpu.CompilerParams(vmem_limit_bytes=VMEM_LIMIT),
        cost_estimate=pl.CostEstimate(flops=flops, bytes_accessed=moved, transcendentals=0),
        name=name,
    )


def iotas(rows, lanes=BLK):
    return (
        lax.broadcasted_iota(jnp.int32, (rows, lanes), 0),
        lax.broadcasted_iota(jnp.int32, (rows, lanes), 1),
    )


def split(x):
    hi = x.astype(BF16)
    lo = (x - hi.astype(F32)).astype(BF16)
    return hi, lo


def dot(a, b, ca=1, cb=0):
    return lax.dot_general(a, b, (((ca,), (cb,)), ((), ())), preferred_element_type=F32)


def dot_exact(a, b, ca=1, cb=0):
    return lax.dot_general(
        a, b, (((ca,), (cb,)), ((), ())), preferred_element_type=F32, precision=highest
    )


def rows_times_bf16(x, b, cb=0):
    hi, lo = split(x)
    both = dot(jnp.concatenate([hi, lo], axis=0), b, 1, cb)
    n = x.shape[0]
    return both[:n] + both[n:]


def stacked(b):
    hi, lo = split(b)
    return jnp.concatenate(
        [
            jnp.concatenate([hi, lo], axis=1),
            jnp.concatenate([hi, jnp.zeros_like(hi)], axis=1),
        ],
        axis=0,
    )


def dot_wide(a, b):
    hi, lo = split(a)
    out = dot(jnp.concatenate([hi, lo], axis=1), stacked(b))
    return out[:, :BLK] + out[:, BLK:]


def pair(b, axis):
    return jnp.concatenate(split(b), axis=axis)


def dot_pair(a, b, cb=0):
    n = a.shape[0]
    out = dot(pair(a, 0), b, 1, cb)
    return out[:n, :BLK] + (out[n:, :BLK] + out[:n, BLK:] + out[n:, BLK:])


def side_by_side(c, b):
    return jnp.concatenate([c[b, m] for m in range(3)], axis=1)


def eliminate(packs):
    sub, lane = iotas(8)
    start = lane - lane % SEG
    parts = [[p[8 * t : 8 * t + 8] for t in range(SEG // 8)] for p in packs]
    for k in range(SEG - 1, -1, -STEP):
        i = k // 8
        spots = [k % 8 - b for b in range(STEP)]
        index = [start + (k - b) for b in range(STEP)]
        at = [lane == x for x in index]
        for part in parts:
            cols = [
                [jnp.take_along_axis(part[t], x, axis=1, mode="promise_in_bounds") for x in index]
                for t in range(i + 1)
            ]
            pivot = [
                [jnp.broadcast_to(c[spots[b] : spots[b] + 1], (8, BLK)) for c in cols[i]]
                for b in range(STEP)
            ]
            ratio = [[None] * STEP for _ in range(STEP)]
            final, scaled = [], []
            for b in range(STEP):
                row = jnp.broadcast_to(part[i][spots[b] : spots[b] + 1], (8, BLK))
                for a in range(b):
                    row = row - pivot[a][b] * scaled[a]
                    for c in range(b, STEP):
                        pivot[b][c] = pivot[b][c] - ratio[a][b] * pivot[a][c]
                root = lax.rsqrt(pivot[b][b])
                inverse = root * root
                for c in range(b + 1, STEP):
                    ratio[b][c] = inverse * pivot[b][c]
                final.append(jnp.where(at[b], root, row * root))
                scaled.append(jnp.where(at[b], 1.0 + inverse, row * inverse))
            for t in range(i):
                new = part[t]
                for b in range(STEP):
                    col = cols[t][b]
                    for a in range(b):
                        col = col - cols[t][a] * ratio[a][b]
                    cols[t][b] = col
                    new = new - col * scaled[b]
                part[t] = new
            for b in range(STEP):
                part[i] = jnp.where(sub == spots[b], final[b], part[i])
    return [jnp.concatenate(part, axis=0) for part in parts]


def factor(z, count):
    sub, lane = iotas(SEG)
    seg = lane // SEG
    groups = -(-count // GROUP)
    for kb in range(GROUP - 1, -1, -1):
        r0 = kb * SEG
        panels = [
            [z[min(q * GROUP + g, count - 1), r0 : r0 + SEG, :] for g in range(GROUP)]
            for q in range(groups)
        ]
        packs = []
        for q in range(groups):
            pack = jnp.zeros((SEG, BLK), F32)
            for g in range(GROUP):
                shift = (SEG * g - r0) % BLK
                x = panels[q][g]
                x = pltpu.roll(x, shift, 1) if shift else x
                pack = jnp.where(seg == g, x, pack)
            packs.append(pack)
        packs = eliminate(packs)
        eye = (lane - r0 == sub).astype(F32)
        for q in range(groups):
            w = jnp.where(lane % SEG >= sub, packs[q], 0.0)
            wide = jnp.concatenate([jnp.where(seg == g, w, 0.0) for g in range(GROUP)], axis=0)
            tall = jnp.concatenate(
                [jnp.where(seg == kb, eye, panels[q][g]) for g in range(GROUP)], axis=0
            )
            v = dot_wide(wide, tall)
            if kb:
                v2 = dot_wide(wide.T, v)
            for g in range(GROUP):
                b = q * GROUP + g
                if b >= count:
                    continue
                z[b, r0 : r0 + SEG, :] = v[SEG * g : SEG * g + SEG]
                if kb:
                    pads = [jnp.zeros((r0, BLK), F32), v2[SEG * g : SEG * g + SEG]]
                    if r0 + SEG < BLK:
                        pads.append(jnp.zeros((BLK - r0 - SEG, BLK), F32))
                    top = z[b, 0:r0, :]
                    update = dot_wide(top, jnp.concatenate(pads, axis=0))
                    _, top_lane = iotas(r0)
                    z[b, 0:r0, :] = jnp.where(top_lane // SEG == kb, 0.0, top) - update


def build_diag(noise, shift, b, factor_value):
    sub, lane = iotas(BLK)
    n = noise[b]
    eye = (sub == lane).astype(BF16)
    turned = dot(eye, n, 1, 1)
    sym = (n.astype(F32) + turned) * (0.5 * factor_value)
    shift_row = shift[pl.ds(b, 1), :].astype(F32)
    return sym + jnp.where(sub == lane, shift_row, 0.0)


def route_kernel(me_ref, dev_ref, slot_ref, ask_ref, pos_ref, chip_ref, count_ref):
    n_dev = count_ref.shape[0]
    me = me_ref[0]

    def clear(t, carry):
        count_ref[t] = 0
        return carry

    lax.fori_loop(0, n_dev, clear, 0, unroll=32)
    _, lane = iotas(8, n_dev)
    codes = jnp.zeros((8, n_dev), jnp.int32)
    for i in range(dev_ref.shape[1]):
        for m in range(3):
            t = me - 1 - dev_ref[m, i]
            t = jnp.where(t < 0, t + n_dev, t)
            rank = count_ref[t]
            count_ref[t] = rank + 1
            code = slot_ref[m, i] + 1
            code = jnp.where(rank == 0, code, code * CODE)
            codes = codes + jnp.where(lane == t, code, 0)
            pos_ref[i * 3 + m] = t * SLOTS + rank
    for q in range(3 * dev_ref.shape[1]):
        at = pos_ref[q]
        t = at // SLOTS
        core = t % CORES
        chip_ref[q] = at + core * (count_ref[t - core] - SLOTS)
    for t in range(n_dev // 8):
        ask_ref[8 * t : 8 * t + 8, :] = codes


def crowd_kernel(table, crowd):
    n_dev = table.shape[1]
    asked = (table[...] > 0).astype(F32) + (table[...] >= CODE).astype(F32)
    _, device = iotas(n_dev, n_dev)
    shared = jnp.where(device % CORES == 0, asked + pltpu.roll(asked, n_dev - 1, 1), 0.0)
    crowd[0] = (jnp.max(shared) > SLOTS + 1.5).astype(jnp.int32)


def invert_kernel(factor_value, noise, shift, x_out, pay_out, z):
    count = noise.shape[0]
    for b in range(count):
        z[b] = build_diag(noise, shift, b, factor_value)
    factor(z, count)
    sub, lane = iotas(BLK)
    top_sub, top_lane = iotas(TRI)
    low_eye = (top_lane == top_sub + TRI).astype(BF16)
    tail_sub, _ = iotas(TAIL)
    for b in range(count):
        x = jnp.where(lane >= sub, z[b], 0.0)
        x_out[b] = x
        bottom = jnp.concatenate([x[TRI:].astype(BF16), jnp.zeros((TRI, BLK), BF16)], axis=0)
        turned = dot(low_eye, bottom, 1, 1)
        tri = jnp.where(top_lane > top_sub, x[:TRI], jnp.where(top_lane < top_sub, turned, 0.0))
        pay_out[b, :TRI] = tri.astype(BF16)
        diag = jnp.sum(jnp.where(sub == lane, x, 0.0), axis=0, keepdims=True)
        hi, lo = split(diag)
        hi, lo = hi.astype(F32), lo.astype(F32)
        for r in range(SLOTS):
            tail = jnp.where(
                tail_sub == 2 * r, hi, jnp.where(tail_sub == 2 * r + 1, lo, 0.0)
            )
            pay_out[b, TRI + r * TAIL : TRI + (r + 1) * TAIL] = tail.astype(BF16)


def serve_kernel(me_ref, incoming, pay, out):
    me = me_ref[0]

    def one(t, carry):
        code = incoming[t, me]
        slots = [jnp.maximum(code % CODE - 1, 0), jnp.maximum(code // CODE - 1, 0)]
        for r in range(SLOTS):
            out[t, r * TRI : (r + 1) * TRI] = pay[slots[r], :TRI]
        out[t, SLOTS * TRI :] = pay[slots[0], TRI : TRI + TAIL] + pay[slots[1], TRI + TAIL :]
        return carry

    lax.fori_loop(0, out.shape[0], one, 0, unroll=8)


def serve_chip_kernel(me_ref, incoming, own, sibling, out, pay):
    me = me_ref[0]
    core = me % CORES
    pay[core] = own[...]
    pay[1 - core] = sibling[...]
    half = pl.multiple_of(core * HALF, HALF)

    def one(t, carry):
        low = incoming[t, me - core]
        high = incoming[t, me - core + 1]
        first, second = low % CODE, low // CODE
        third, fourth = high % CODE, high // CODE
        none, one_low = first == 0, second == 0
        mine_core = jnp.where(core == 0, none, one_low).astype(jnp.int32)
        mine = jnp.where(
            core == 0,
            jnp.where(none, third, first),
            jnp.where(none, fourth, jnp.where(one_low, third, second)),
        )
        mine = jnp.maximum(mine - 1, 0)
        last = jnp.maximum(jnp.where(one_low, fourth, third) - 1, 0)
        out[t, :TRI] = pay[mine_core, mine, :TRI]
        out[t, TRI : TRI + HALF] = pay[1, last, pl.ds(half, HALF)]
        out[t, TRI + HALF :] = pay[mine_core, mine, TRI : TRI + TAIL] + pay[1, last, TRI + TAIL :]
        return carry

    lax.fori_loop(0, out.shape[0], one, 0, unroll=8)


def row_kernel(
    factor_value, coupling_factor, by_chip, pos, chip_pos, noise, shift, couplings, vectors, arrived,
    w_out, y_out, send, z, stage, sems,
):
    count = noise.shape[0]
    n_vec = vectors.shape[0]
    for b in range(count):
        z[b] = build_diag(noise, shift, b, factor_value)
    top_sub, top_lane = iotas(TRI)

    tail_sub, _ = iotas(TAIL)
    zero = jnp.zeros((TRI, BLK), BF16)

    def schur(b, carry):
        wide = []
        for m in range(3):
            q = b * 3 + m
            if by_chip:
                at = chip_pos[q]
                chip, k = at // (CORES * SLOTS), at % (CORES * SLOTS)
                rank = k // SLOTS
                dev = chip * CORES + k % SLOTS
                dev_two = dev + rank
                row = rank * TRI
                row_two = jnp.where(rank == 0, HALF, TRI)
            else:
                at = pos[q]
                dev, rank = at // SLOTS, at % SLOTS
                dev_two = dev
                row = rank * TRI
                row_two = row + HALF
            tri = jnp.concatenate(
                [
                    arrived[dev, pl.ds(pl.multiple_of(row, HALF), HALF), :],
                    arrived[dev_two, pl.ds(pl.multiple_of(row_two, HALF), HALF), :],
                ],
                axis=0,
            ).astype(F32)
            upper = jnp.where(top_lane > top_sub, tri, 0.0).astype(BF16)
            lower = pltpu.roll(jnp.where(top_lane < top_sub, tri, 0.0), TRI, 1).astype(BF16)
            diag = jnp.sum(
                jnp.where(tail_sub // 2 == rank, arrived[dev, arrived.shape[1] - TAIL :, :].astype(F32), 0.0),
                axis=0,
                keepdims=True,
            )
            c = couplings[b, m]
            y = dot(c, jnp.concatenate([upper, zero], axis=0), 1, 1)
            y = y + dot(c, jnp.concatenate([zero, lower], axis=0), 1, 0)
            wide.append((y + c.astype(F32) * diag).astype(BF16))
        wide = jnp.concatenate(wide, axis=1)
        z[b] = z[b] - dot(wide, wide, 1, 1) * (coupling_factor * coupling_factor)
        return carry

    lax.fori_loop(0, count, schur, 0, unroll=7)
    factor(z, count)
    sub, lane = iotas(BLK)
    copies = []
    for b in range(count):
        w = jnp.where(lane >= sub, z[b], 0.0)
        hi, lo = split(w)
        w_out[b] = jnp.concatenate([hi, lo], axis=0)
        y = dot_pair(vectors[:, b * BLK : (b + 1) * BLK], jnp.concatenate([hi, lo], axis=1))
        y_out[b] = y
        p = (rows_times_bf16(y, side_by_side(couplings, b)) * coupling_factor).astype(BF16)
        for m in range(3):
            q = b * 3 + m
            stage[q] = p[:, m * BLK : (m + 1) * BLK]
            copy = pltpu.make_async_copy(stage.at[q], send.at[pos[q]], sems.at[q])
            copy.start()
            copies.append(copy)
    for copy in copies:
        copy.wait()


def between_kernel(
    factor_value, me_ref, incoming, table, x, noise, shift, y,
    e_out, own_out, list_pos, list_slot, list_count, clash,
):
    me = me_ref[0]

    def one(t, n):
        code = incoming[t, me]
        for r in range(SLOTS):
            slot = (code % CODE if r == 0 else code // CODE) - 1
            list_pos[n] = t * SLOTS + r
            list_slot[n] = slot
            n = n + (slot >= 0).astype(jnp.int32)
        return n

    list_count[0] = lax.fori_loop(0, incoming.shape[0], one, 0, unroll=8)
    double = (table[...] >= CODE).astype(F32)
    clash[0] = (jnp.max(double * double.T) > 0.5).astype(jnp.int32)
    for b in range(noise.shape[0]):
        e_out[b] = pair(dot_exact(x[b], x[b], 0, 0), 1)
        d = build_diag(noise, shift, b, factor_value)
        own_out[b] = dot_pair(y[b], pair(d, 1))


def push_slot(slots, rank):
    return SLOTS + rank if slots == 2 * SLOTS else SLOTS - rank


def left_kernel(
    coupling_factor, pos, list_pos, list_slot, list_count, arrived, y, e, couplings, send, left, total
):
    count = y.shape[0]
    total[...] = jnp.zeros_like(total)

    def add(t, carry):
        slot = list_slot[t]
        total[slot] += arrived[list_pos[t]].astype(F32)
        return carry

    lax.fori_loop(0, list_count[0], add, 0)
    for b in range(count):
        u = dot_pair(total[b], e[b])
        left[b] = (y[b] - u).astype(BF16)
        p = (rows_times_bf16(u, side_by_side(couplings, b)) * coupling_factor).astype(BF16)
        for m in range(3):
            at = pos[b * 3 + m]
            send[at // SLOTS, push_slot(send.shape[1], at % SLOTS)] = p[:, m * BLK : (m + 1) * BLK]

    def give(t, carry):
        at = list_pos[t]
        send[at // SLOTS, at % SLOTS] = left[list_slot[t]]
        return carry

    lax.fori_loop(0, list_count[0], give, 0)


def middle_kernel(
    coupling_factor, pos, list_pos, list_slot, list_count, arrived, own, e, couplings,
    middle, send, total, answer,
):
    count = own.shape[0]
    total[...] = jnp.zeros_like(total)

    def add(t, carry):
        slot = list_slot[t]
        at = list_pos[t]
        place = push_slot(arrived.shape[1], at % SLOTS)
        total[slot] += arrived[at // SLOTS, place].astype(F32)
        return carry

    lax.fori_loop(0, list_count[0], add, 0)
    for b in range(count):
        places = [pos[b * 3 + m] for m in range(3)]
        near = jnp.concatenate([arrived[at // SLOTS, at % SLOTS] for at in places], axis=1)
        near = dot(near, side_by_side(couplings, b), 1, 1)
        mid = own[b] - total[b] + near * coupling_factor
        middle[b] = mid
        answer[b] = dot_pair(mid, e[b]).astype(BF16)

    def give(t, carry):
        send[list_pos[t]] = answer[list_slot[t]]
        return carry

    lax.fori_loop(0, list_count[0], give, 0)


def result_kernel(coupling_factor, pos, arrived, middle, w, couplings, out):
    for b in range(middle.shape[0]):
        near = jnp.concatenate([arrived[pos[b * 3 + m]] for m in range(3)], axis=1)
        near = dot(near, side_by_side(couplings, b), 1, 1)
        mid = middle[b] - near * coupling_factor
        out[:, b * BLK : (b + 1) * BLK] = dot_pair(mid, w[b], 1)


def exchange(x):
    return lax.all_to_all(x, "rows", split_axis=0, concat_axis=0, tiled=True)


def body(diag_noise, couplings, shifts, near_devices, near_slots, vectors):
    n_dev = lax.axis_size("rows")
    me = lax.axis_index("rows").astype(jnp.int32).reshape(1)
    count = diag_noise.shape[0]
    n_vec = vectors.shape[0]
    total_slots = n_dev * SLOTS
    factor_value = 0.5 / math.sqrt(BLK)
    coupling_factor = 0.4 / math.sqrt(BLK)

    def shape(dims, dtype=F32):
        return jax.ShapeDtypeStruct(dims, dtype)

    blocks = shape((count, BLK, BLK))
    rows = shape((count, n_vec, BLK))

    def with_factors(kernel, *values):
        def wrapped(*refs):
            kernel(*values, *refs)

        return wrapped

    ask, pos, chip_pos = call(
        route_kernel,
        (
            shape((n_dev, n_dev), jnp.int32),
            shape((3 * count,), jnp.int32),
            shape((3 * count,), jnp.int32),
        ),
        [SM, SM, SM],
        (VM, SM, SM),
        [SM((n_dev,), jnp.int32)],
        name="route",
    )(me, near_devices.T, near_slots.T)
    table = exchange(ask)
    x, pay = call(
        with_factors(invert_kernel, factor_value),
        (blocks, shape((count, PAY, BLK), BF16)),
        [VM, VM],
        (VM, VM),
        [VM((count, BLK, BLK), F32)],
        flops=2 * 10**9,
        moved=10**8,
        name="invert",
    )(diag_noise, shifts)
    pay, table = lax.optimization_barrier((pay, table))
    sibling = lax.ppermute(pay, "rows", [(i, i + 1 - 2 * (i % CORES)) for i in range(n_dev)])
    crowd = call(
        crowd_kernel,
        shape((1,), jnp.int32),
        [VM],
        SM,
        flops=10**8,
        moved=10**6,
        name="crowd",
    )(table)

    def setup(by_chip, me, table, pay, sibling, pos, chip_pos, diag_noise, shifts, couplings, vectors):
        if by_chip:
            answer = call(
                serve_chip_kernel,
                shape((n_dev, TRI + HALF + TAIL, BLK), BF16),
                [SM, SM, VM, VM],
                VM,
                [VM((CORES, count, PAY, BLK), BF16)],
                name="serve",
            )(me, table, pay, sibling)
        else:
            answer = call(
                serve_kernel,
                shape((n_dev, SLOTS * TRI + TAIL, BLK), BF16),
                [SM, SM, VM],
                VM,
                name="serve",
            )(me, table, pay)
        return call(
            with_factors(row_kernel, factor_value, coupling_factor, by_chip),
            (
                shape((count, 2 * BLK, BLK), BF16),
                rows,
                pltpu.HBM((total_slots, n_vec, BLK), BF16),
            ),
            [SM, SM, VM, VM, VM, VM, VM],
            (VM, VM, pltpu.HBM),
            [
                VM((count, BLK, BLK), F32),
                VM((3 * count, n_vec, BLK), BF16),
                pltpu.SemaphoreType.DMA((3 * count,)),
            ],
            name="row",
        )(pos, chip_pos, diag_noise, shifts, couplings, vectors, exchange(answer))

    w, y, push = lax.cond(
        crowd[0] > 0,
        functools.partial(setup, False),
        functools.partial(setup, True),
        me, table, pay, sibling, pos, chip_pos, diag_noise, shifts, couplings, vectors,
    )
    pushed = exchange(push.reshape(n_dev, SLOTS * n_vec, BLK)).reshape(total_slots, n_vec, BLK)
    e, own, *lists, clash = call(
        with_factors(between_kernel, factor_value),
        (
            shape((count, BLK, 2 * BLK), BF16),
            rows,
            shape((total_slots + SLOTS,), jnp.int32),
            shape((total_slots + SLOTS,), jnp.int32),
            shape((1,), jnp.int32),
            shape((1,), jnp.int32),
        ),
        [SM, SM] + [VM] * 5,
        (VM, VM, SM, SM, SM, SM),
        flops=2 * 10**9,
        moved=10**7,
        name="between",
    )(me, table, table, x, diag_noise, shifts, y)

    def swap(slots, pos, lists, pushed, y, e, own, couplings):
        both = call(
            with_factors(left_kernel, coupling_factor),
            shape((n_dev, slots, n_vec, BLK), BF16),
            [SM] * 4 + [VM] * 4,
            VM,
            [VM((count, n_vec, BLK), BF16), VM((count, n_vec, BLK), F32)],
            name="left",
        )(pos, *lists, pushed, y, e, couplings)
        both = exchange(both.reshape(n_dev, slots * n_vec, BLK)).reshape(
            n_dev, slots, n_vec, BLK
        )
        return call(
            with_factors(middle_kernel, coupling_factor),
            (rows, shape((total_slots, n_vec, BLK), BF16)),
            [SM] * 4 + [VM] * 4,
            (VM, VM),
            [VM((count, n_vec, BLK), F32), VM((count, n_vec, BLK), BF16)],
            name="middle",
        )(pos, *lists, both, own, e, couplings)

    middle, back = lax.cond(
        clash[0] > 0,
        functools.partial(swap, 2 * SLOTS),
        functools.partial(swap, 2 * SLOTS - 1),
        pos, lists, pushed, y, e, own, couplings,
    )
    back = exchange(back.reshape(n_dev, SLOTS * n_vec, BLK)).reshape(total_slots, n_vec, BLK)
    return call(
        with_factors(result_kernel, coupling_factor),
        shape((n_vec, count * BLK)),
        [SM] + [VM] * 4,
        VM,
        name="result",
    )(pos, back, middle, w, couplings)


def solution(mesh):
    return jax.shard_map(
        body,
        mesh=mesh,
        in_specs=(
            P("rows", None, None),
            P("rows", None, None, None),
            P("rows", None),
            P("rows", None),
            P("rows", None),
            P(None, "rows"),
        ),
        out_specs=P(None, "rows"),
        check_vma=False,
    )
```

```python
import functools
import math

import jax
import jax.numpy as jnp
from jax import lax
from jax.experimental import pallas as pl
from jax.experimental.pallas import tpu as pltpu
from jax.sharding import PartitionSpec as P

F32 = jnp.float32
BF16 = jnp.bfloat16
BLK = 128
SLOTS = 2
CORES = 2
TRI = 64
TAIL = 16
HALF = TRI // 2
PAY = TRI + SLOTS * TAIL
SEG = 16
STEP = 8
GROUP = BLK // SEG
CODE = 16
VMEM_LIMIT = 16 * 1024 * 1024
SM = pltpu.SMEM
VM = pltpu.VMEM
highest = lax.Precision.HIGHEST


def spec(space):
    return pl.BlockSpec(memory_space=space)


def call(kernel, out_shape, ins, outs, scratch=(), flops=0, moved=0, name=None):
    return pl.pallas_call(
        kernel,
        out_shape=out_shape,
        in_specs=[spec(s) for s in ins],
        out_specs=jax.tree.map(spec, outs),
        scratch_shapes=list(scratch),
        compiler_params=pltpu.CompilerParams(vmem_limit_bytes=VMEM_LIMIT),
        cost_estimate=pl.CostEstimate(flops=flops, bytes_accessed=moved, transcendentals=0),
        name=name,
    )


def whole(x, n):
    return lax.shift_right_logical(x, jnp.int32(n.bit_length() - 1))


def rest(x, n):
    return x & (n - 1)


def iotas(rows, lanes=BLK):
    return (
        lax.broadcasted_iota(jnp.int32, (rows, lanes), 0),
        lax.broadcasted_iota(jnp.int32, (rows, lanes), 1),
    )


def split(x):
    hi = x.astype(BF16)
    lo = (x - hi.astype(F32)).astype(BF16)
    return hi, lo


def dot(a, b, ca=1, cb=0):
    return lax.dot_general(a, b, (((ca,), (cb,)), ((), ())), preferred_element_type=F32)


def dot_exact(a, b, ca=1, cb=0):
    return lax.dot_general(
        a, b, (((ca,), (cb,)), ((), ())), preferred_element_type=F32, precision=highest
    )


def rows_times_bf16(x, b, cb=0):
    hi, lo = split(x)
    both = dot(jnp.concatenate([hi, lo], axis=0), b, 1, cb)
    n = x.shape[0]
    return both[:n] + both[n:]


def stacked(b):
    hi, lo = split(b)
    return jnp.concatenate(
        [
            jnp.concatenate([hi, lo], axis=1),
            jnp.concatenate([hi, jnp.zeros_like(hi)], axis=1),
        ],
        axis=0,
    )


def dot_wide(a, b):
    hi, lo = split(a)
    out = dot(jnp.concatenate([hi, lo], axis=1), stacked(b))
    return out[:, :BLK] + out[:, BLK:]


def pair(b, axis):
    return jnp.concatenate(split(b), axis=axis)


def dot_pair(a, b, cb=0):
    n = a.shape[0]
    out = dot(pair(a, 0), b, 1, cb)
    return out[:n, :BLK] + (out[n:, :BLK] + out[:n, BLK:] + out[n:, BLK:])


def side_by_side(c, b):
    return jnp.concatenate([c[b, m] for m in range(3)], axis=1)


def eliminate(packs):
    sub, lane = iotas(8)
    start = lane - rest(lane, SEG)
    parts = [[p[8 * t : 8 * t + 8] for t in range(SEG // 8)] for p in packs]
    for k in range(SEG - 1, -1, -STEP):
        i = k // 8
        spots = [k % 8 - b for b in range(STEP)]
        index = [start + (k - b) for b in range(STEP)]
        at = [lane == x for x in index]
        for part in parts:
            cols = [
                [jnp.take_along_axis(part[t], x, axis=1, mode="promise_in_bounds") for x in index]
                for t in range(i + 1)
            ]
            pivot = [
                [jnp.broadcast_to(c[spots[b] : spots[b] + 1], (8, BLK)) for c in cols[i]]
                for b in range(STEP)
            ]
            ratio = [[None] * STEP for _ in range(STEP)]
            final, scaled = [], []
            for b in range(STEP):
                row = jnp.broadcast_to(part[i][spots[b] : spots[b] + 1], (8, BLK))
                for a in range(b):
                    row = row - pivot[a][b] * scaled[a]
                    for c in range(b, STEP):
                        pivot[b][c] = pivot[b][c] - ratio[a][b] * pivot[a][c]
                root = lax.rsqrt(pivot[b][b])
                inverse = root * root
                for c in range(b + 1, STEP):
                    ratio[b][c] = inverse * pivot[b][c]
                final.append(jnp.where(at[b], root, row * root))
                scaled.append(jnp.where(at[b], 1.0 + inverse, row * inverse))
            for t in range(i):
                new = part[t]
                for b in range(STEP):
                    col = cols[t][b]
                    for a in range(b):
                        col = col - cols[t][a] * ratio[a][b]
                    cols[t][b] = col
                    new = new - col * scaled[b]
                part[t] = new
            for b in range(STEP):
                part[i] = jnp.where(sub == spots[b], final[b], part[i])
    return [jnp.concatenate(part, axis=0) for part in parts]


def factor(z, count):
    sub, lane = iotas(SEG)
    seg = whole(lane, SEG)
    groups = -(-count // GROUP)
    for kb in range(GROUP - 1, -1, -1):
        r0 = kb * SEG
        panels = [
            [z[min(q * GROUP + g, count - 1), r0 : r0 + SEG, :] for g in range(GROUP)]
            for q in range(groups)
        ]
        packs = []
        for q in range(groups):
            pack = jnp.zeros((SEG, BLK), F32)
            for g in range(GROUP):
                shift = (SEG * g - r0) % BLK
                x = panels[q][g]
                x = pltpu.roll(x, shift, 1) if shift else x
                pack = jnp.where(seg == g, x, pack)
            packs.append(pack)
        packs = eliminate(packs)
        eye = (lane - r0 == sub).astype(F32)
        for q in range(groups):
            w = jnp.where(rest(lane, SEG) >= sub, packs[q], 0.0)
            wide = jnp.concatenate([jnp.where(seg == g, w, 0.0) for g in range(GROUP)], axis=0)
            tall = jnp.concatenate(
                [jnp.where(seg == kb, eye, panels[q][g]) for g in range(GROUP)], axis=0
            )
            v = dot_wide(wide, tall)
            if kb:
                v2 = dot_wide(wide.T, v)
            for g in range(GROUP):
                b = q * GROUP + g
                if b >= count:
                    continue
                z[b, r0 : r0 + SEG, :] = v[SEG * g : SEG * g + SEG]
                if kb:
                    pads = [jnp.zeros((r0, BLK), F32), v2[SEG * g : SEG * g + SEG]]
                    if r0 + SEG < BLK:
                        pads.append(jnp.zeros((BLK - r0 - SEG, BLK), F32))
                    top = z[b, 0:r0, :]
                    update = dot_wide(top, jnp.concatenate(pads, axis=0))
                    _, top_lane = iotas(r0)
                    z[b, 0:r0, :] = jnp.where((top_lane >= r0) & (top_lane < r0 + SEG), 0.0, top) - update


def build_diag(noise, shift, b, factor_value):
    sub, lane = iotas(BLK)
    n = noise[b]
    eye = (sub == lane).astype(BF16)
    turned = dot(eye, n, 1, 1)
    sym = (n.astype(F32) + turned) * (0.5 * factor_value)
    shift_row = shift[pl.ds(b, 1), :].astype(F32)
    return sym + jnp.where(sub == lane, shift_row, 0.0)


def route_kernel(me_ref, dev_ref, slot_ref, ask_ref, pos_ref, chip_ref, count_ref):
    n_dev = count_ref.shape[0]
    me = me_ref[0]

    def clear(t, carry):
        count_ref[t] = 0
        return carry

    lax.fori_loop(0, n_dev, clear, 0, unroll=32)
    _, lane = iotas(8, n_dev)
    codes = jnp.zeros((8, n_dev), jnp.int32)
    for i in range(dev_ref.shape[1]):
        for m in range(3):
            t = me - 1 - dev_ref[m, i]
            t = jnp.where(t < 0, t + n_dev, t)
            rank = count_ref[t]
            count_ref[t] = rank + 1
            code = slot_ref[m, i] + 1
            code = jnp.where(rank == 0, code, code * CODE)
            codes = codes + jnp.where(lane == t, code, 0)
            pos_ref[i * 3 + m] = t * SLOTS + rank
    for q in range(3 * dev_ref.shape[1]):
        at = pos_ref[q]
        t = whole(at, SLOTS)
        core = rest(t, CORES)
        chip_ref[q] = at + core * (count_ref[t - core] - SLOTS)
    for t in range(n_dev // 8):
        ask_ref[8 * t : 8 * t + 8, :] = codes


def crowd_kernel(table, crowd):
    n_dev = table.shape[1]
    asked = (table[...] > 0).astype(F32) + (table[...] >= CODE).astype(F32)
    _, device = iotas(n_dev, n_dev)
    shared = jnp.where(rest(device, CORES) == 0, asked + pltpu.roll(asked, n_dev - 1, 1), 0.0)
    crowd[0] = (jnp.max(shared) > SLOTS + 1.5).astype(jnp.int32)


def invert_kernel(factor_value, noise, shift, x_out, pay_out, z):
    count = noise.shape[0]
    for b in range(count):
        z[b] = build_diag(noise, shift, b, factor_value)
    factor(z, count)
    sub, lane = iotas(BLK)
    top_sub, top_lane = iotas(TRI)
    low_eye = (top_lane == top_sub + TRI).astype(BF16)
    tail_sub, _ = iotas(TAIL)
    for b in range(count):
        x = jnp.where(lane >= sub, z[b], 0.0)
        x_out[b] = x
        bottom = jnp.concatenate([x[TRI:].astype(BF16), jnp.zeros((TRI, BLK), BF16)], axis=0)
        turned = dot(low_eye, bottom, 1, 1)
        tri = jnp.where(top_lane > top_sub, x[:TRI], jnp.where(top_lane < top_sub, turned, 0.0))
        pay_out[b, :TRI] = tri.astype(BF16)
        diag = jnp.sum(jnp.where(sub == lane, x, 0.0), axis=0, keepdims=True)
        hi, lo = split(diag)
        hi, lo = hi.astype(F32), lo.astype(F32)
        for r in range(SLOTS):
            tail = jnp.where(
                tail_sub == 2 * r, hi, jnp.where(tail_sub == 2 * r + 1, lo, 0.0)
            )
            pay_out[b, TRI + r * TAIL : TRI + (r + 1) * TAIL] = tail.astype(BF16)


def serve_kernel(me_ref, incoming, pay, out):
    me = me_ref[0]

    def one(t, carry):
        code = incoming[t, me]
        slots = [jnp.maximum(rest(code, CODE) - 1, 0), jnp.maximum(whole(code, CODE) - 1, 0)]
        for r in range(SLOTS):
            out[t, r * TRI : (r + 1) * TRI] = pay[slots[r], :TRI]
        out[t, SLOTS * TRI :] = pay[slots[0], TRI : TRI + TAIL] + pay[slots[1], TRI + TAIL :]
        return carry

    lax.fori_loop(0, out.shape[0], one, 0, unroll=8)


def serve_chip_kernel(me_ref, incoming, own, sibling, out, pay):
    me = me_ref[0]
    core = rest(me, CORES)
    pay[core] = own[...]
    pay[1 - core] = sibling[...]
    half = pl.multiple_of(core * HALF, HALF)

    def one(t, carry):
        low = incoming[t, me - core]
        high = incoming[t, me - core + 1]
        first, second = rest(low, CODE), whole(low, CODE)
        third, fourth = rest(high, CODE), whole(high, CODE)
        none, one_low = first == 0, second == 0
        mine_core = jnp.where(core == 0, none, one_low).astype(jnp.int32)
        mine = jnp.where(
            core == 0,
            jnp.where(none, third, first),
            jnp.where(none, fourth, jnp.where(one_low, third, second)),
        )
        mine = jnp.maximum(mine - 1, 0)
        last = jnp.maximum(jnp.where(one_low, fourth, third) - 1, 0)
        out[t, :TRI] = pay[mine_core, mine, :TRI]
        out[t, TRI : TRI + HALF] = pay[1, last, pl.ds(half, HALF)]
        out[t, TRI + HALF :] = pay[mine_core, mine, TRI : TRI + TAIL] + pay[1, last, TRI + TAIL :]
        return carry

    lax.fori_loop(0, out.shape[0], one, 0, unroll=8)


def row_kernel(
    factor_value, coupling_factor, by_chip, pos, chip_pos, noise, shift, couplings, vectors, arrived,
    w_out, y_out, send, z, stage, sems,
):
    count = noise.shape[0]
    n_vec = vectors.shape[0]
    for b in range(count):
        z[b] = build_diag(noise, shift, b, factor_value)
    top_sub, top_lane = iotas(TRI)

    tail_sub, _ = iotas(TAIL)
    zero = jnp.zeros((TRI, BLK), BF16)

    def schur(b, carry):
        wide = []
        for m in range(3):
            q = b * 3 + m
            if by_chip:
                at = chip_pos[q]
                chip, k = whole(at, CORES * SLOTS), rest(at, CORES * SLOTS)
                rank = whole(k, SLOTS)
                dev = chip * CORES + rest(k, SLOTS)
                dev_two = dev + rank
                row = rank * TRI
                row_two = jnp.where(rank == 0, HALF, TRI)
            else:
                at = pos[q]
                dev, rank = whole(at, SLOTS), rest(at, SLOTS)
                dev_two = dev
                row = rank * TRI
                row_two = row + HALF
            tri = jnp.concatenate(
                [
                    arrived[dev, pl.ds(pl.multiple_of(row, HALF), HALF), :],
                    arrived[dev_two, pl.ds(pl.multiple_of(row_two, HALF), HALF), :],
                ],
                axis=0,
            ).astype(F32)
            upper = jnp.where(top_lane > top_sub, tri, 0.0).astype(BF16)
            lower = pltpu.roll(jnp.where(top_lane < top_sub, tri, 0.0), TRI, 1).astype(BF16)
            diag = jnp.sum(
                jnp.where(whole(tail_sub, SLOTS) == rank, arrived[dev, arrived.shape[1] - TAIL :, :].astype(F32), 0.0),
                axis=0,
                keepdims=True,
            )
            c = couplings[b, m]
            y = dot(c, jnp.concatenate([upper, zero], axis=0), 1, 1)
            y = y + dot(c, jnp.concatenate([zero, lower], axis=0), 1, 0)
            wide.append((y + c.astype(F32) * diag).astype(BF16))
        wide = jnp.concatenate(wide, axis=1)
        z[b] = z[b] - dot(wide, wide, 1, 1) * (coupling_factor * coupling_factor)
        return carry

    lax.fori_loop(0, count, schur, 0, unroll=7)
    factor(z, count)
    sub, lane = iotas(BLK)
    copies = []
    for b in range(count):
        w = jnp.where(lane >= sub, z[b], 0.0)
        hi, lo = split(w)
        w_out[b] = jnp.concatenate([hi, lo], axis=0)
        y = dot_pair(vectors[:, b * BLK : (b + 1) * BLK], jnp.concatenate([hi, lo], axis=1))
        y_out[b] = y
        p = (rows_times_bf16(y, side_by_side(couplings, b)) * coupling_factor).astype(BF16)
        for m in range(3):
            q = b * 3 + m
            stage[q] = p[:, m * BLK : (m + 1) * BLK]
            copy = pltpu.make_async_copy(stage.at[q], send.at[pos[q]], sems.at[q])
            copy.start()
            copies.append(copy)
    for copy in copies:
        copy.wait()


def between_kernel(
    factor_value, me_ref, incoming, table, x, noise, shift, y,
    e_out, own_out, list_pos, list_slot, list_count, clash,
):
    me = me_ref[0]

    def one(t, n):
        code = incoming[t, me]
        for r in range(SLOTS):
            slot = (rest(code, CODE) if r == 0 else whole(code, CODE)) - 1
            list_pos[n] = t * SLOTS + r
            list_slot[n] = slot
            n = n + (slot >= 0).astype(jnp.int32)
        return n

    list_count[0] = lax.fori_loop(0, incoming.shape[0], one, 0, unroll=8)
    double = (table[...] >= CODE).astype(F32)
    clash[0] = (jnp.max(double * double.T) > 0.5).astype(jnp.int32)
    for b in range(noise.shape[0]):
        e_out[b] = pair(dot_exact(x[b], x[b], 0, 0), 1)
        d = build_diag(noise, shift, b, factor_value)
        own_out[b] = dot_pair(y[b], pair(d, 1))


def push_slot(slots, rank):
    return SLOTS + rank if slots == 2 * SLOTS else SLOTS - rank


def left_kernel(
    coupling_factor, pos, list_pos, list_slot, list_count, arrived, y, e, couplings, send, left, total
):
    count = y.shape[0]
    total[...] = jnp.zeros_like(total)

    def add(t, carry):
        slot = list_slot[t]
        total[slot] += arrived[list_pos[t]].astype(F32)
        return carry

    lax.fori_loop(0, list_count[0], add, 0)
    for b in range(count):
        u = dot_pair(total[b], e[b])
        left[b] = (y[b] - u).astype(BF16)
        p = (rows_times_bf16(u, side_by_side(couplings, b)) * coupling_factor).astype(BF16)
        for m in range(3):
            at = pos[b * 3 + m]
            send[whole(at, SLOTS), push_slot(send.shape[1], rest(at, SLOTS))] = p[:, m * BLK : (m + 1) * BLK]

    def give(t, carry):
        at = list_pos[t]
        send[whole(at, SLOTS), rest(at, SLOTS)] = left[list_slot[t]]
        return carry

    lax.fori_loop(0, list_count[0], give, 0)


def middle_kernel(
    coupling_factor, pos, list_pos, list_slot, list_count, arrived, own, e, couplings,
    middle, send, total, answer,
):
    count = own.shape[0]
    total[...] = jnp.zeros_like(total)

    def add(t, carry):
        slot = list_slot[t]
        at = list_pos[t]
        place = push_slot(arrived.shape[1], rest(at, SLOTS))
        total[slot] += arrived[whole(at, SLOTS), place].astype(F32)
        return carry

    lax.fori_loop(0, list_count[0], add, 0)
    for b in range(count):
        places = [pos[b * 3 + m] for m in range(3)]
        near = jnp.concatenate([arrived[whole(at, SLOTS), rest(at, SLOTS)] for at in places], axis=1)
        near = dot(near, side_by_side(couplings, b), 1, 1)
        mid = own[b] - total[b] + near * coupling_factor
        middle[b] = mid
        answer[b] = dot_pair(mid, e[b]).astype(BF16)

    def give(t, carry):
        send[list_pos[t]] = answer[list_slot[t]]
        return carry

    lax.fori_loop(0, list_count[0], give, 0)


def result_kernel(coupling_factor, pos, arrived, middle, w, couplings, out):
    for b in range(middle.shape[0]):
        near = jnp.concatenate([arrived[pos[b * 3 + m]] for m in range(3)], axis=1)
        near = dot(near, side_by_side(couplings, b), 1, 1)
        mid = middle[b] - near * coupling_factor
        out[:, b * BLK : (b + 1) * BLK] = dot_pair(mid, w[b], 1)


def exchange(x):
    return lax.all_to_all(x, "rows", split_axis=0, concat_axis=0, tiled=True)


def body(diag_noise, couplings, shifts, near_devices, near_slots, vectors):
    n_dev = lax.axis_size("rows")
    me = lax.axis_index("rows").astype(jnp.int32).reshape(1)
    count = diag_noise.shape[0]
    n_vec = vectors.shape[0]
    total_slots = n_dev * SLOTS
    factor_value = 0.5 / math.sqrt(BLK)
    coupling_factor = 0.4 / math.sqrt(BLK)

    def shape(dims, dtype=F32):
        return jax.ShapeDtypeStruct(dims, dtype)

    blocks = shape((count, BLK, BLK))
    rows = shape((count, n_vec, BLK))

    def with_factors(kernel, *values):
        def wrapped(*refs):
            kernel(*values, *refs)

        return wrapped

    ask, pos, chip_pos = call(
        route_kernel,
        (
            shape((n_dev, n_dev), jnp.int32),
            shape((3 * count,), jnp.int32),
            shape((3 * count,), jnp.int32),
        ),
        [SM, SM, SM],
        (VM, SM, SM),
        [SM((n_dev,), jnp.int32)],
        name="route",
    )(
        me,
        pltpu.with_memory_space_constraint(near_devices.T, pltpu.HBM),
        pltpu.with_memory_space_constraint(near_slots.T, pltpu.HBM),
    )
    table = exchange(ask)
    x, pay = call(
        with_factors(invert_kernel, factor_value),
        (blocks, shape((count, PAY, BLK), BF16)),
        [VM, VM],
        (VM, VM),
        [VM((count, BLK, BLK), F32)],
        flops=2 * 10**9,
        moved=10**8,
        name="invert",
    )(diag_noise, shifts)
    pay, table = lax.optimization_barrier((pay, table))
    sibling = lax.ppermute(pay, "rows", [(i, i + 1 - 2 * (i % CORES)) for i in range(n_dev)])
    crowd = call(
        crowd_kernel,
        shape((1,), jnp.int32),
        [VM],
        SM,
        flops=10**8,
        moved=10**6,
        name="crowd",
    )(table)

    def setup(by_chip, me, table, pay, sibling, pos, chip_pos, diag_noise, shifts, couplings, vectors):
        if by_chip:
            answer = call(
                serve_chip_kernel,
                shape((n_dev, TRI + HALF + TAIL, BLK), BF16),
                [SM, SM, VM, VM],
                VM,
                [VM((CORES, count, PAY, BLK), BF16)],
                name="serve",
            )(me, table, pay, sibling)
        else:
            answer = call(
                serve_kernel,
                shape((n_dev, SLOTS * TRI + TAIL, BLK), BF16),
                [SM, SM, VM],
                VM,
                name="serve",
            )(me, table, pay)
        return call(
            with_factors(row_kernel, factor_value, coupling_factor, by_chip),
            (
                shape((count, 2 * BLK, BLK), BF16),
                rows,
                pltpu.HBM((total_slots, n_vec, BLK), BF16),
            ),
            [SM, SM, VM, VM, VM, VM, VM],
            (VM, VM, pltpu.HBM),
            [
                VM((count, BLK, BLK), F32),
                VM((3 * count, n_vec, BLK), BF16),
                pltpu.SemaphoreType.DMA((3 * count,)),
            ],
            name="row",
        )(pos, chip_pos, diag_noise, shifts, couplings, vectors, exchange(answer))

    w, y, push = lax.cond(
        crowd[0] > 0,
        functools.partial(setup, False),
        functools.partial(setup, True),
        me, table, pay, sibling, pos, chip_pos, diag_noise, shifts, couplings, vectors,
    )
    pushed = exchange(push.reshape(n_dev, SLOTS * n_vec, BLK)).reshape(total_slots, n_vec, BLK)
    e, own, *lists, clash = call(
        with_factors(between_kernel, factor_value),
        (
            shape((count, BLK, 2 * BLK), BF16),
            rows,
            shape((total_slots + SLOTS,), jnp.int32),
            shape((total_slots + SLOTS,), jnp.int32),
            shape((1,), jnp.int32),
            shape((1,), jnp.int32),
        ),
        [SM, SM] + [VM] * 5,
        (VM, VM, SM, SM, SM, SM),
        flops=2 * 10**9,
        moved=10**7,
        name="between",
    )(me, table, table, x, diag_noise, shifts, y)

    def swap(slots, pos, lists, pushed, y, e, own, couplings):
        both = call(
            with_factors(left_kernel, coupling_factor),
            shape((n_dev, slots, n_vec, BLK), BF16),
            [SM] * 4 + [VM] * 4,
            VM,
            [VM((count, n_vec, BLK), BF16), VM((count, n_vec, BLK), F32)],
            name="left",
        )(pos, *lists, pushed, y, e, couplings)
        both = exchange(both.reshape(n_dev, slots * n_vec, BLK)).reshape(
            n_dev, slots, n_vec, BLK
        )
        return call(
            with_factors(middle_kernel, coupling_factor),
            (rows, shape((total_slots, n_vec, BLK), BF16)),
            [SM] * 4 + [VM] * 4,
            (VM, VM),
            [VM((count, n_vec, BLK), F32), VM((count, n_vec, BLK), BF16)],
            name="middle",
        )(pos, *lists, both, own, e, couplings)

    middle, back = lax.cond(
        clash[0] > 0,
        functools.partial(swap, 2 * SLOTS),
        functools.partial(swap, 2 * SLOTS - 1),
        pos, lists, pushed, y, e, own, couplings,
    )
    back = exchange(back.reshape(n_dev, SLOTS * n_vec, BLK)).reshape(total_slots, n_vec, BLK)
    return call(
        with_factors(result_kernel, coupling_factor),
        shape((n_vec, count * BLK)),
        [SM] + [VM] * 4,
        VM,
        name="result",
    )(pos, back, middle, w, couplings)


def solution(mesh):
    return jax.shard_map(
        body,
        mesh=mesh,
        in_specs=(
            P("rows", None, None),
            P("rows", None, None, None),
            P("rows", None),
            P("rows", None),
            P("rows", None),
            P(None, "rows"),
        ),
        out_specs=P(None, "rows"),
        check_vma=False,
    )
```

```python
import functools
import math

import jax
import jax.numpy as jnp
from jax import lax
from jax.experimental import pallas as pl
from jax.experimental.pallas import tpu as pltpu
from jax.sharding import PartitionSpec as P

F32 = jnp.float32
BF16 = jnp.bfloat16
BLK = 128
SLOTS = 2
CORES = 2
TRI = 64
TAIL = 16
HALF = TRI // 2
PAY = TRI + SLOTS * TAIL
SEG = 16
STEP = 8
GROUP = BLK // SEG
CODE = 16
VMEM_LIMIT = 16 * 1024 * 1024
SM = pltpu.SMEM
VM = pltpu.VMEM
highest = lax.Precision.HIGHEST


def spec(space):
    return pl.BlockSpec(memory_space=space)


def call(kernel, out_shape, ins, outs, scratch=(), flops=0, moved=0, name=None):
    return pl.pallas_call(
        kernel,
        out_shape=out_shape,
        in_specs=[spec(s) for s in ins],
        out_specs=jax.tree.map(spec, outs),
        scratch_shapes=list(scratch),
        compiler_params=pltpu.CompilerParams(vmem_limit_bytes=VMEM_LIMIT),
        cost_estimate=pl.CostEstimate(flops=flops, bytes_accessed=moved, transcendentals=0),
        name=name,
    )


def whole(x, n):
    return lax.shift_right_logical(x, jnp.int32(n.bit_length() - 1))


def rest(x, n):
    return x & (n - 1)


def iotas(rows, lanes=BLK):
    return (
        lax.broadcasted_iota(jnp.int32, (rows, lanes), 0),
        lax.broadcasted_iota(jnp.int32, (rows, lanes), 1),
    )


def split(x):
    hi = x.astype(BF16)
    lo = (x - hi.astype(F32)).astype(BF16)
    return hi, lo


def dot(a, b, ca=1, cb=0):
    return lax.dot_general(a, b, (((ca,), (cb,)), ((), ())), preferred_element_type=F32)


def dot_exact(a, b, ca=1, cb=0):
    return lax.dot_general(
        a, b, (((ca,), (cb,)), ((), ())), preferred_element_type=F32, precision=highest
    )


def rows_times_bf16(x, b, cb=0):
    hi, lo = split(x)
    both = dot(jnp.concatenate([hi, lo], axis=0), b, 1, cb)
    n = x.shape[0]
    return both[:n] + both[n:]


def stacked(b):
    hi, lo = split(b)
    return jnp.concatenate(
        [
            jnp.concatenate([hi, lo], axis=1),
            jnp.concatenate([hi, jnp.zeros_like(hi)], axis=1),
        ],
        axis=0,
    )


def dot_wide(a, b):
    hi, lo = split(a)
    out = dot(jnp.concatenate([hi, lo], axis=1), stacked(b))
    return out[:, :BLK] + out[:, BLK:]


def pair(b, axis):
    return jnp.concatenate(split(b), axis=axis)


def dot_pair(a, b, cb=0):
    n = a.shape[0]
    out = dot(pair(a, 0), b, 1, cb)
    return out[:n, :BLK] + (out[n:, :BLK] + out[:n, BLK:] + out[n:, BLK:])


def side_by_side(c, b):
    return jnp.concatenate([c[b, m] for m in range(3)], axis=1)


def eliminate(packs):
    sub, lane = iotas(8)
    start = lane - rest(lane, SEG)
    parts = [[p[8 * t : 8 * t + 8] for t in range(SEG // 8)] for p in packs]
    for k in range(SEG - 1, -1, -STEP):
        i = k // 8
        spots = [k % 8 - b for b in range(STEP)]
        index = [start + (k - b) for b in range(STEP)]
        at = [lane == x for x in index]
        for part in parts:
            cols = [
                [jnp.take_along_axis(part[t], x, axis=1, mode="promise_in_bounds") for x in index]
                for t in range(i + 1)
            ]
            pivot = [
                [jnp.broadcast_to(c[spots[b] : spots[b] + 1], (8, BLK)) for c in cols[i]]
                for b in range(STEP)
            ]
            ratio = [[None] * STEP for _ in range(STEP)]
            final, scaled = [], []
            for b in range(STEP):
                row = jnp.broadcast_to(part[i][spots[b] : spots[b] + 1], (8, BLK))
                for a in range(b):
                    row = row - pivot[a][b] * scaled[a]
                    for c in range(b, STEP):
                        pivot[b][c] = pivot[b][c] - ratio[a][b] * pivot[a][c]
                root = lax.rsqrt(pivot[b][b])
                inverse = root * root
                for c in range(b + 1, STEP):
                    ratio[b][c] = inverse * pivot[b][c]
                final.append(jnp.where(at[b], root, row * root))
                scaled.append(jnp.where(at[b], 1.0 + inverse, row * inverse))
            for t in range(i):
                new = part[t]
                for b in range(STEP):
                    col = cols[t][b]
                    for a in range(b):
                        col = col - cols[t][a] * ratio[a][b]
                    cols[t][b] = col
                    new = new - col * scaled[b]
                part[t] = new
            for b in range(STEP):
                part[i] = jnp.where(sub == spots[b], final[b], part[i])
    return [jnp.concatenate(part, axis=0) for part in parts]


def factor(z, count):
    sub, lane = iotas(SEG)
    seg = whole(lane, SEG)
    groups = -(-count // GROUP)
    for kb in range(GROUP - 1, -1, -1):
        r0 = kb * SEG
        panels = [
            [z[min(q * GROUP + g, count - 1), r0 : r0 + SEG, :] for g in range(GROUP)]
            for q in range(groups)
        ]
        packs = []
        for q in range(groups):
            pack = jnp.zeros((SEG, BLK), F32)
            for g in range(GROUP):
                shift = (SEG * g - r0) % BLK
                x = panels[q][g]
                x = pltpu.roll(x, shift, 1) if shift else x
                pack = jnp.where(seg == g, x, pack)
            packs.append(pack)
        packs = eliminate(packs)
        eye = (lane - r0 == sub).astype(F32)
        for q in range(groups):
            w = jnp.where(rest(lane, SEG) >= sub, packs[q], 0.0)
            wide = jnp.concatenate([jnp.where(seg == g, w, 0.0) for g in range(GROUP)], axis=0)
            tall = jnp.concatenate(
                [jnp.where(seg == kb, eye, panels[q][g]) for g in range(GROUP)], axis=0
            )
            v = dot_wide(wide, tall)
            if kb:
                v2 = dot_wide(wide.T, v)
            for g in range(GROUP):
                b = q * GROUP + g
                if b >= count:
                    continue
                z[b, r0 : r0 + SEG, :] = v[SEG * g : SEG * g + SEG]
                if kb:
                    pads = [jnp.zeros((r0, BLK), F32), v2[SEG * g : SEG * g + SEG]]
                    if r0 + SEG < BLK:
                        pads.append(jnp.zeros((BLK - r0 - SEG, BLK), F32))
                    top = z[b, 0:r0, :]
                    update = dot_wide(top, jnp.concatenate(pads, axis=0))
                    _, top_lane = iotas(r0)
                    z[b, 0:r0, :] = jnp.where((top_lane >= r0) & (top_lane < r0 + SEG), 0.0, top) - update


def build_diag(noise, shift, b, factor_value):
    sub, lane = iotas(BLK)
    n = noise[b]
    eye = (sub == lane).astype(BF16)
    turned = dot(eye, n, 1, 1)
    sym = (n.astype(F32) + turned) * (0.5 * factor_value)
    shift_row = shift[pl.ds(b, 1), :].astype(F32)
    return sym + jnp.where(sub == lane, shift_row, 0.0)


def route_kernel(me_ref, dev_ref, slot_ref, ask_ref, pos_ref, chip_ref, count_ref):
    n_dev = count_ref.shape[0]
    me = me_ref[0]

    def clear(t, carry):
        count_ref[t] = 0
        return carry

    lax.fori_loop(0, n_dev, clear, 0, unroll=32)
    _, lane = iotas(8, n_dev)
    codes = jnp.zeros((8, n_dev), jnp.int32)
    for i in range(dev_ref.shape[1]):
        for m in range(3):
            t = me - 1 - dev_ref[m, i]
            t = jnp.where(t < 0, t + n_dev, t)
            rank = count_ref[t]
            count_ref[t] = rank + 1
            code = slot_ref[m, i] + 1
            code = jnp.where(rank == 0, code, code * CODE)
            codes = codes + jnp.where(lane == t, code, 0)
            pos_ref[i * 3 + m] = t * SLOTS + rank
    for q in range(3 * dev_ref.shape[1]):
        at = pos_ref[q]
        t = whole(at, SLOTS)
        core = rest(t, CORES)
        chip_ref[q] = at + core * (count_ref[t - core] - SLOTS)
    for t in range(n_dev // 8):
        ask_ref[8 * t : 8 * t + 8, :] = codes


def crowd_kernel(table, crowd):
    n_dev = table.shape[1]
    asked = (table[...] > 0).astype(F32) + (table[...] >= CODE).astype(F32)
    _, device = iotas(n_dev, n_dev)
    shared = jnp.where(rest(device, CORES) == 0, asked + pltpu.roll(asked, n_dev - 1, 1), 0.0)
    crowd[0] = (jnp.max(shared) > SLOTS + 1.5).astype(jnp.int32)


def invert_kernel(factor_value, noise, shift, x_out, pay_out, z):
    count = noise.shape[0]
    for b in range(count):
        z[b] = build_diag(noise, shift, b, factor_value)
    factor(z, count)
    sub, lane = iotas(BLK)
    top_sub, top_lane = iotas(TRI)
    low_eye = (top_lane == top_sub + TRI).astype(BF16)
    tail_sub, _ = iotas(TAIL)
    for b in range(count):
        x = jnp.where(lane >= sub, z[b], 0.0)
        x_out[b] = x
        bottom = jnp.concatenate([x[TRI:].astype(BF16), jnp.zeros((TRI, BLK), BF16)], axis=0)
        turned = dot(low_eye, bottom, 1, 1)
        tri = jnp.where(top_lane > top_sub, x[:TRI], jnp.where(top_lane < top_sub, turned, 0.0))
        pay_out[b, :TRI] = tri.astype(BF16)
        diag = jnp.sum(jnp.where(sub == lane, x, 0.0), axis=0, keepdims=True)
        hi, lo = split(diag)
        hi, lo = hi.astype(F32), lo.astype(F32)
        for r in range(SLOTS):
            tail = jnp.where(
                tail_sub == 2 * r, hi, jnp.where(tail_sub == 2 * r + 1, lo, 0.0)
            )
            pay_out[b, TRI + r * TAIL : TRI + (r + 1) * TAIL] = tail.astype(BF16)


def serve_kernel(me_ref, incoming, pay, out):
    me = me_ref[0]

    def one(t, carry):
        code = incoming[t, me]
        slots = [jnp.maximum(rest(code, CODE) - 1, 0), jnp.maximum(whole(code, CODE) - 1, 0)]
        for r in range(SLOTS):
            out[t, r * TRI : (r + 1) * TRI] = pay[slots[r], :TRI]
        out[t, SLOTS * TRI :] = pay[slots[0], TRI : TRI + TAIL] + pay[slots[1], TRI + TAIL :]
        return carry

    lax.fori_loop(0, out.shape[0], one, 0, unroll=16)


def serve_chip_kernel(me_ref, incoming, own, sibling, out, pay):
    me = me_ref[0]
    core = rest(me, CORES)
    pay[core] = own[...]
    pay[1 - core] = sibling[...]
    half = pl.multiple_of(core * HALF, HALF)

    def one(t, carry):
        low = incoming[t, me - core]
        high = incoming[t, me - core + 1]
        first, second = rest(low, CODE), whole(low, CODE)
        third, fourth = rest(high, CODE), whole(high, CODE)
        none, one_low = first == 0, second == 0
        mine_core = jnp.where(core == 0, none, one_low).astype(jnp.int32)
        mine = jnp.where(
            core == 0,
            jnp.where(none, third, first),
            jnp.where(none, fourth, jnp.where(one_low, third, second)),
        )
        mine = jnp.maximum(mine - 1, 0)
        last = jnp.maximum(jnp.where(one_low, fourth, third) - 1, 0)
        out[t, :TRI] = pay[mine_core, mine, :TRI]
        out[t, TRI : TRI + HALF] = pay[1, last, pl.ds(half, HALF)]
        out[t, TRI + HALF :] = pay[mine_core, mine, TRI : TRI + TAIL] + pay[1, last, TRI + TAIL :]
        return carry

    lax.fori_loop(0, out.shape[0], one, 0, unroll=16)


def row_kernel(
    factor_value, coupling_factor, by_chip, pos, chip_pos, noise, shift, couplings, vectors, arrived,
    w_out, y_out, send, z, stage, sems,
):
    count = noise.shape[0]
    n_vec = vectors.shape[0]
    for b in range(count):
        z[b] = build_diag(noise, shift, b, factor_value)
    top_sub, top_lane = iotas(TRI)

    tail_sub, _ = iotas(TAIL)
    zero = jnp.zeros((TRI, BLK), BF16)

    def schur(b, carry):
        wide = []
        for m in range(3):
            q = b * 3 + m
            if by_chip:
                at = chip_pos[q]
                chip, k = whole(at, CORES * SLOTS), rest(at, CORES * SLOTS)
                rank = whole(k, SLOTS)
                dev = chip * CORES + rest(k, SLOTS)
                dev_two = dev + rank
                row = rank * TRI
                row_two = jnp.where(rank == 0, HALF, TRI)
            else:
                at = pos[q]
                dev, rank = whole(at, SLOTS), rest(at, SLOTS)
                dev_two = dev
                row = rank * TRI
                row_two = row + HALF
            tri = jnp.concatenate(
                [
                    arrived[dev, pl.ds(pl.multiple_of(row, HALF), HALF), :],
                    arrived[dev_two, pl.ds(pl.multiple_of(row_two, HALF), HALF), :],
                ],
                axis=0,
            ).astype(F32)
            upper = jnp.where(top_lane > top_sub, tri, 0.0).astype(BF16)
            lower = pltpu.roll(jnp.where(top_lane < top_sub, tri, 0.0), TRI, 1).astype(BF16)
            diag = jnp.sum(
                jnp.where(whole(tail_sub, SLOTS) == rank, arrived[dev, arrived.shape[1] - TAIL :, :].astype(F32), 0.0),
                axis=0,
                keepdims=True,
            )
            c = couplings[b, m]
            y = dot(c, jnp.concatenate([upper, zero], axis=0), 1, 1)
            y = y + dot(c, jnp.concatenate([zero, lower], axis=0), 1, 0)
            wide.append((y + c.astype(F32) * diag).astype(BF16))
        wide = jnp.concatenate(wide, axis=1)
        z[b] = z[b] - dot(wide, wide, 1, 1) * (coupling_factor * coupling_factor)
        return carry

    lax.fori_loop(0, count, schur, 0, unroll=14)
    factor(z, count)
    sub, lane = iotas(BLK)
    copies = []
    for b in range(count):
        w = jnp.where(lane >= sub, z[b], 0.0)
        hi, lo = split(w)
        w_out[b] = jnp.concatenate([hi, lo], axis=0)
        y = dot_pair(vectors[:, b * BLK : (b + 1) * BLK], jnp.concatenate([hi, lo], axis=1))
        y_out[b] = y
        p = (rows_times_bf16(y, side_by_side(couplings, b)) * coupling_factor).astype(BF16)
        for m in range(3):
            q = b * 3 + m
            stage[q] = p[:, m * BLK : (m + 1) * BLK]
            copy = pltpu.make_async_copy(stage.at[q], send.at[pos[q]], sems.at[q])
            copy.start()
            copies.append(copy)
    for copy in copies:
        copy.wait()


def between_kernel(
    factor_value, me_ref, incoming, table, x, noise, shift, y,
    e_out, own_out, list_pos, list_slot, list_count, clash,
):
    me = me_ref[0]

    def one(t, n):
        code = incoming[t, me]
        for r in range(SLOTS):
            slot = (rest(code, CODE) if r == 0 else whole(code, CODE)) - 1
            list_pos[n] = t * SLOTS + r
            list_slot[n] = slot
            n = n + (slot >= 0).astype(jnp.int32)
        return n

    list_count[0] = lax.fori_loop(0, incoming.shape[0], one, 0, unroll=8)
    double = (table[...] >= CODE).astype(F32)
    clash[0] = (jnp.max(double * double.T) > 0.5).astype(jnp.int32)
    for b in range(noise.shape[0]):
        e_out[b] = pair(dot_exact(x[b], x[b], 0, 0), 1)
        d = build_diag(noise, shift, b, factor_value)
        own_out[b] = dot_pair(y[b], pair(d, 1))


def push_slot(slots, rank):
    return SLOTS + rank if slots == 2 * SLOTS else SLOTS - rank


def left_kernel(
    coupling_factor, pos, list_pos, list_slot, list_count, arrived, y, e, couplings, send, left, total
):
    count = y.shape[0]
    total[...] = jnp.zeros_like(total)

    def add(t, carry):
        slot = list_slot[t]
        total[slot] += arrived[list_pos[t]].astype(F32)
        return carry

    lax.fori_loop(0, list_count[0], add, 0)
    for b in range(count):
        u = dot_pair(total[b], e[b])
        left[b] = (y[b] - u).astype(BF16)
        p = (rows_times_bf16(u, side_by_side(couplings, b)) * coupling_factor).astype(BF16)
        for m in range(3):
            at = pos[b * 3 + m]
            send[whole(at, SLOTS), push_slot(send.shape[1], rest(at, SLOTS))] = p[:, m * BLK : (m + 1) * BLK]

    def give(t, carry):
        at = list_pos[t]
        send[whole(at, SLOTS), rest(at, SLOTS)] = left[list_slot[t]]
        return carry

    lax.fori_loop(0, list_count[0], give, 0)


def middle_kernel(
    coupling_factor, pos, list_pos, list_slot, list_count, arrived, own, e, couplings,
    middle, send, total, answer,
):
    count = own.shape[0]
    total[...] = jnp.zeros_like(total)

    def add(t, carry):
        slot = list_slot[t]
        at = list_pos[t]
        place = push_slot(arrived.shape[1], rest(at, SLOTS))
        total[slot] += arrived[whole(at, SLOTS), place].astype(F32)
        return carry

    lax.fori_loop(0, list_count[0], add, 0)
    for b in range(count):
        places = [pos[b * 3 + m] for m in range(3)]
        near = jnp.concatenate([arrived[whole(at, SLOTS), rest(at, SLOTS)] for at in places], axis=1)
        near = dot(near, side_by_side(couplings, b), 1, 1)
        mid = own[b] - total[b] + near * coupling_factor
        middle[b] = mid
        answer[b] = dot_pair(mid, e[b]).astype(BF16)

    def give(t, carry):
        send[list_pos[t]] = answer[list_slot[t]]
        return carry

    lax.fori_loop(0, list_count[0], give, 0)


def result_kernel(coupling_factor, pos, arrived, middle, w, couplings, out):
    for b in range(middle.shape[0]):
        near = jnp.concatenate([arrived[pos[b * 3 + m]] for m in range(3)], axis=1)
        near = dot(near, side_by_side(couplings, b), 1, 1)
        mid = middle[b] - near * coupling_factor
        out[:, b * BLK : (b + 1) * BLK] = dot_pair(mid, w[b], 1)


def exchange(x):
    return lax.all_to_all(x, "rows", split_axis=0, concat_axis=0, tiled=True)


def body(diag_noise, couplings, shifts, near_devices, near_slots, vectors):
    n_dev = lax.axis_size("rows")
    me = lax.axis_index("rows").astype(jnp.int32).reshape(1)
    count = diag_noise.shape[0]
    n_vec = vectors.shape[0]
    total_slots = n_dev * SLOTS
    factor_value = 0.5 / math.sqrt(BLK)
    coupling_factor = 0.4 / math.sqrt(BLK)

    def shape(dims, dtype=F32):
        return jax.ShapeDtypeStruct(dims, dtype)

    blocks = shape((count, BLK, BLK))
    rows = shape((count, n_vec, BLK))

    def with_factors(kernel, *values):
        def wrapped(*refs):
            kernel(*values, *refs)

        return wrapped

    ask, pos, chip_pos = call(
        route_kernel,
        (
            shape((n_dev, n_dev), jnp.int32),
            shape((3 * count,), jnp.int32),
            shape((3 * count,), jnp.int32),
        ),
        [SM, SM, SM],
        (VM, SM, SM),
        [SM((n_dev,), jnp.int32)],
        name="route",
    )(
        me,
        pltpu.with_memory_space_constraint(near_devices.T, pltpu.HBM),
        pltpu.with_memory_space_constraint(near_slots.T, pltpu.HBM),
    )
    table = exchange(ask)
    x, pay = call(
        with_factors(invert_kernel, factor_value),
        (blocks, shape((count, PAY, BLK), BF16)),
        [VM, VM],
        (VM, VM),
        [VM((count, BLK, BLK), F32)],
        flops=2 * 10**9,
        moved=10**8,
        name="invert",
    )(diag_noise, shifts)
    pay, table = lax.optimization_barrier((pay, table))
    sibling = lax.ppermute(pay, "rows", [(i, i + 1 - 2 * (i % CORES)) for i in range(n_dev)])
    crowd = call(
        crowd_kernel,
        shape((1,), jnp.int32),
        [VM],
        SM,
        flops=10**8,
        moved=10**6,
        name="crowd",
    )(table)

    def setup(by_chip, me, table, pay, sibling, pos, chip_pos, diag_noise, shifts, couplings, vectors):
        if by_chip:
            answer = call(
                serve_chip_kernel,
                shape((n_dev, TRI + HALF + TAIL, BLK), BF16),
                [SM, SM, VM, VM],
                VM,
                [VM((CORES, count, PAY, BLK), BF16)],
                name="serve",
            )(me, table, pay, sibling)
        else:
            answer = call(
                serve_kernel,
                shape((n_dev, SLOTS * TRI + TAIL, BLK), BF16),
                [SM, SM, VM],
                VM,
                name="serve",
            )(me, table, pay)
        return call(
            with_factors(row_kernel, factor_value, coupling_factor, by_chip),
            (
                shape((count, 2 * BLK, BLK), BF16),
                rows,
                pltpu.HBM((total_slots, n_vec, BLK), BF16),
            ),
            [SM, SM, VM, VM, VM, VM, VM],
            (VM, VM, pltpu.HBM),
            [
                VM((count, BLK, BLK), F32),
                VM((3 * count, n_vec, BLK), BF16),
                pltpu.SemaphoreType.DMA((3 * count,)),
            ],
            name="row",
        )(pos, chip_pos, diag_noise, shifts, couplings, vectors, exchange(answer))

    w, y, push = lax.cond(
        crowd[0] > 0,
        functools.partial(setup, False),
        functools.partial(setup, True),
        me, table, pay, sibling, pos, chip_pos, diag_noise, shifts, couplings, vectors,
    )
    pushed = exchange(push.reshape(n_dev, SLOTS * n_vec, BLK)).reshape(total_slots, n_vec, BLK)
    e, own, *lists, clash = call(
        with_factors(between_kernel, factor_value),
        (
            shape((count, BLK, 2 * BLK), BF16),
            rows,
            shape((total_slots + SLOTS,), jnp.int32),
            shape((total_slots + SLOTS,), jnp.int32),
            shape((1,), jnp.int32),
            shape((1,), jnp.int32),
        ),
        [SM, SM] + [VM] * 5,
        (VM, VM, SM, SM, SM, SM),
        flops=2 * 10**9,
        moved=10**7,
        name="between",
    )(me, table, table, x, diag_noise, shifts, y)

    def swap(slots, pos, lists, pushed, y, e, own, couplings):
        both = call(
            with_factors(left_kernel, coupling_factor),
            shape((n_dev, slots, n_vec, BLK), BF16),
            [SM] * 4 + [VM] * 4,
            VM,
            [VM((count, n_vec, BLK), BF16), VM((count, n_vec, BLK), F32)],
            name="left",
        )(pos, *lists, pushed, y, e, couplings)
        both = exchange(both.reshape(n_dev, slots * n_vec, BLK)).reshape(
            n_dev, slots, n_vec, BLK
        )
        return call(
            with_factors(middle_kernel, coupling_factor),
            (rows, shape((total_slots, n_vec, BLK), BF16)),
            [SM] * 4 + [VM] * 4,
            (VM, VM),
            [VM((count, n_vec, BLK), F32), VM((count, n_vec, BLK), BF16)],
            name="middle",
        )(pos, *lists, both, own, e, couplings)

    middle, back = lax.cond(
        clash[0] > 0,
        functools.partial(swap, 2 * SLOTS),
        functools.partial(swap, 2 * SLOTS - 1),
        pos, lists, pushed, y, e, own, couplings,
    )
    back = exchange(back.reshape(n_dev, SLOTS * n_vec, BLK)).reshape(total_slots, n_vec, BLK)
    return call(
        with_factors(result_kernel, coupling_factor),
        shape((n_vec, count * BLK)),
        [SM] + [VM] * 4,
        VM,
        name="result",
    )(pos, back, middle, w, couplings)


def solution(mesh):
    return jax.shard_map(
        body,
        mesh=mesh,
        in_specs=(
            P("rows", None, None),
            P("rows", None, None, None),
            P("rows", None),
            P("rows", None),
            P("rows", None),
            P(None, "rows"),
        ),
        out_specs=P(None, "rows"),
        check_vma=False,
    )
```
